256 devices in a mesh: seq: 32 (over z, y), chan: 8 (over x, core).
Axes of the slice: x: 4, y: 4, z: 8, core: 2. Of those that a mesh axis runs over, the one named last changes fastest.
Arguments:
- query: bfloat16 [16384, 4096], P('seq', 'chan'), may hold values from -6 to 6
- key_stream: bfloat16 [16384, 4096], P('seq', 'chan'), may hold values from -6 to 6
- value: bfloat16 [16384, 4096], P('seq', 'chan'), may hold values from -6 to 6
- long_filter: float32 [16384, 4096], P('seq', 'chan'), may hold values from -0.046875 to 0.046875
- w_out: bfloat16 [4096, 4096], P('chan'), may hold values from -0.125 to 0.125
Outputs:
- mixed: bfloat16 [16384, 4096], P('seq', 'chan')
The draws below stay inside these ranges and needn't reach their ends.
All inputs are finite; a program needn't handle non-finite values.
Results may differ from the reference program's by a relative error of at most 0.005.
Values sent between devices are 32-bit elements; how exact they have to be, the bound alone decides.
No kernel may reach another device: no remote copies, remote signals or barrier semaphores. Data moves between devices by JAX's collectives and lax.ppermute only.
A program may use at most 128 MiB of HBM per device.

```python
import jax
import jax.numpy as jnp
from jax import lax

D = 4096
TOKENS = 16384


def raised(array, key, source, target, parts, factor):
    owner, partner = [(jnp.arange(array.shape[axis_at]) // (array.shape[axis_at] // parts)).reshape([-1 if axis == axis_at else 1 for axis in range(array.ndim)]) for axis_at in (source, target)]
    chosen = jax.random.permutation(key, parts)[partner]
    strong = (owner == chosen) | (owner == (partner + parts // 2) % parts)
    return jnp.where(strong, factor * array, array)


def block_levels(stream_key, dims, cuts, smallest, top_value):
    factor_of = 1.0
    for position, parts in cuts:
        heights = jax.random.uniform(jax.random.fold_in(jax.random.fold_in(stream_key, 6), position), (parts,), jnp.float32, smallest / len(cuts), top_value / len(cuts))
        factor_of = factor_of * jnp.repeat(jnp.exp(heights), dims[position] // parts).reshape((-1,) + (1,) * (len(dims) - 1 - position))
    return factor_of


def noise(stream_key, shape, deviation, bound, cuts=(), kind=jnp.bfloat16):
    entries = jax.random.normal(stream_key, shape, jnp.float32) * deviation
    if len(cuts) > 0:
        entries = block_levels(stream_key, shape, cuts, -0.22, 0.18) * entries
    return jnp.clip(entries, min=-bound, max=bound).astype(kind)


def heavy_noise(rng, dims, spread, reach, pieces, heavy, dtype=jnp.bfloat16):
    drawn = spread * jax.random.normal(rng, dims, jnp.float32)
    if pieces:
        drawn = drawn * block_levels(rng, dims, pieces, -0.22, 0.18)
    return jnp.clip(raised(drawn, jax.random.fold_in(rng, 3), *heavy), -reach, reach).astype(dtype)


def setup_inputs(seed: int = 0) -> dict:
    seeds = jax.random.split(jax.random.key(seed), 6)
    return {
        "query": noise(seeds[0], (TOKENS, D), 1.0, 6.0, ((0, 32), (1, 8))),
        "key_stream": noise(seeds[1], (TOKENS, D), 1.0, 6.0, ((0, 32), (1, 8))),
        "value": noise(seeds[2], (TOKENS, D), 1.0, 6.0, ((0, 32), (1, 8))),
        "long_filter": noise(seeds[3], (TOKENS, D), TOKENS ** -0.5, 0.046875, ((0, 32), (1, 8)), jnp.float32),
        "w_out": heavy_noise(seeds[4], (D, D), D ** -0.5, 0.125, ((0, 8),), (0, 1, 8, 2.0)),
    }


def reference(query, key_stream, value, long_filter, w_out):
    signal = key_stream.astype(jnp.float32) * value.astype(jnp.float32)
    padded = 2 * TOKENS
    group = min(D, 256)
    signal_cols = signal.T.reshape(D // group, group, TOKENS)
    filter_cols = long_filter.T.reshape(D // group, group, TOKENS)

    def convolve(pair):
        spectrum = jnp.fft.rfft(pair[0], n=padded, axis=-1) * jnp.fft.rfft(pair[1], n=padded, axis=-1)
        return jnp.fft.irfft(spectrum, n=padded, axis=-1)[:, :TOKENS]

    conv = lax.map(convolve, (signal_cols, filter_cols)).reshape(D, TOKENS).T
    gated = (query.astype(jnp.float32) * conv).astype(jnp.bfloat16)
    return jnp.dot(gated, w_out, preferred_element_type=jnp.float32).astype(jnp.bfloat16)
```

```python
import functools

import jax
import jax.numpy as jnp
import numpy as np
from jax import lax
from jax.experimental import pallas as pl
from jax.experimental.pallas import tpu as pltpu
from jax.sharding import PartitionSpec as P

LANES = 128
COARSE = 128
TOTAL = 2 * COARSE * LANES
PEERS = 32
OWN = 16
SUB = 4


def split_bf16(x):
    high = x.astype(jnp.bfloat16)
    low = (x - high.astype(jnp.float32)).astype(jnp.bfloat16)
    return high, low


def np_split(x):
    x = np.asarray(x, np.float32)
    high = x.astype(jnp.bfloat16)
    low = (x - high.astype(np.float32)).astype(jnp.bfloat16)
    return high, low


def tables():
    k = np.arange(COARSE)
    q = np.arange(COARSE)
    r = np.arange(LANES)
    coarse = 2.0 * np.pi * ((k[:, None] * q[None, :]) % (2 * COARSE)) / (2 * COARSE)
    first = np.concatenate([np.cos(coarse), -np.sin(coarse)], 0)
    fine = 2.0 * np.pi * ((r[:, None] * r[None, :]) % LANES) / LANES
    cos_f, sin_f = np.cos(fine), np.sin(fine)
    second = np.block([[cos_f, -sin_f], [sin_f, cos_f]])
    second_inv = np.block([[cos_f, sin_f], [-sin_f, cos_f]])
    weight = np.where(k == 0, 1.0, 2.0)[None, :] / TOTAL
    last = np.concatenate([weight * np.cos(coarse.T), -weight * np.sin(coarse.T)], 1)
    twist = 2.0 * np.pi * ((k[:, None] * r[None, :]) % TOTAL) / TOTAL
    middle = 2.0 * np.pi * (COARSE * r) / TOTAL
    edge = np.stack([np.cos(middle), np.sin(middle)], 0)
    sign = np.broadcast_to(np.where(q % 2 == 0, 1.0, -1.0)[:, None] / TOTAL, (COARSE, LANES))
    first_h, first_l = np_split(first)
    out = [np.concatenate([first_h, first_h], 1), first_l]
    for matrix in (second, second_inv, last):
        out.extend(np_split(matrix))
    f32 = lambda x: np.ascontiguousarray(x).astype(np.float32)
    out.extend([f32(np.cos(twist)), f32(np.sin(twist)), f32(edge), f32(sign)])
    return out


def prepare_kernel(key_ref, value_ref, taps_ref, out_ref):
    signal = key_ref[...].astype(jnp.float32) * value_ref[...].astype(jnp.float32)
    taps = taps_ref[...]
    groups = LANES // OWN
    for e in range(SUB):
        rows = slice(e * LANES, (e + 1) * LANES)
        for s, stream in enumerate((signal, taps)):
            at = (2 * e + s) * OWN
            out_ref[:, at:at + OWN, :] = stream[rows, :].T.reshape(groups, OWN, LANES)


def prepare(key_stream, value, taps):
    rows, channels = key_stream.shape
    block = pl.BlockSpec((rows, LANES), lambda i: (0, i))
    return pl.pallas_call(
        prepare_kernel,
        grid=(channels // LANES,),
        in_specs=[block, block, block],
        out_specs=pl.BlockSpec((LANES // OWN, 2 * SUB * OWN, LANES), lambda i: (i, 0, 0)),
        out_shape=jax.ShapeDtypeStruct((PEERS, 2 * SUB * OWN, LANES), jnp.float32),
        compiler_params=pltpu.CompilerParams(vmem_limit_bytes=32 * 1024 * 1024),
        cost_estimate=pl.CostEstimate(flops=0, bytes_accessed=4 << 20, transcendentals=0),
    )(key_stream, value, taps)


def dot(a, b):
    return jnp.dot(a, b, preferred_element_type=jnp.float32)


def dot3(a, b_high, b_low):
    a_high, a_low = split_bf16(a)
    return dot(a_high, b_high) + dot(a_low, b_high) + dot(a_high, b_low)


def convolve_kernel(
    x_ref, first2, first_l, second_h, second_l, inverse_h, inverse_l, last_h, last_l,
    cos_ref, sin_ref, edge_ref, sign_ref, out_ref, edge_out,
):
    def add_pair(i, total):
        at = pl.multiple_of(i * (4 * OWN), 4 * OWN)
        return total + (x_ref[pl.ds(at, 2 * OWN), :] - x_ref[pl.ds(at + 2 * OWN, 2 * OWN), :])

    half = lax.fori_loop(
        0, COARSE // 2, add_pair, jnp.zeros((2 * OWN, LANES), jnp.float32), unroll=8
    )
    edge_cos, edge_sin = edge_ref[0:1, :], edge_ref[1:2, :]
    spun = jnp.concatenate([half * edge_cos, -half * edge_sin], 1)
    spectrum = dot3(spun, second_h[...], second_l[...])
    sig, fil = spectrum[:OWN], spectrum[OWN:]
    sr, si, fr, fi = sig[:, :LANES], sig[:, LANES:], fil[:, :LANES], fil[:, LANES:]
    product = jnp.concatenate([sr * fr - si * fi, sr * fi + si * fr], 1)
    back = dot3(product, inverse_h[...], inverse_l[...])
    edge_out[...] = back[:, :LANES] * edge_cos - back[:, LANES:] * edge_sin

    def pair(i, carry):
        c0 = 2 * i
        streams = [
            x_ref[pl.ds(s * OWN + c0 + j, COARSE, stride=2 * OWN), :]
            for j in range(2) for s in range(2)
        ]
        x = jnp.concatenate(streams, 1)
        x_h, x_l = split_bf16(x)
        y = dot(first2[...], jnp.concatenate([x_h, x_l], 0)) + dot(first_l[...], x_h)
        cos, sin = cos_ref[...], sin_ref[...]
        turned = []
        for j in range(4):
            yr = y[:COARSE, j * LANES:(j + 1) * LANES]
            yi = y[COARSE:, j * LANES:(j + 1) * LANES]
            turned.append(jnp.concatenate([yr * cos + yi * sin, yi * cos - yr * sin], 1))
        z = dot3(jnp.concatenate(turned, 0), second_h[...], second_l[...])
        products = []
        for j in range(2):
            sig = z[2 * j * COARSE:(2 * j + 1) * COARSE]
            fil = z[(2 * j + 1) * COARSE:(2 * j + 2) * COARSE]
            sr, si, fr, fi = sig[:, :LANES], sig[:, LANES:], fil[:, :LANES], fil[:, LANES:]
            products.append(jnp.concatenate([sr * fr - si * fi, sr * fi + si * fr], 1))
        u = dot3(jnp.concatenate(products, 0), inverse_h[...], inverse_l[...])
        columns = []
        for j in range(2):
            ur = u[j * COARSE:(j + 1) * COARSE, :LANES]
            ui = u[j * COARSE:(j + 1) * COARSE, LANES:]
            columns.append(jnp.concatenate([ur * cos - ui * sin, ur * sin + ui * cos], 0))
        v_h, v_l = split_bf16(jnp.concatenate(columns, 1))
        result = dot(last_h[...], v_h) + dot(last_h[...], v_l) + dot(last_l[...], v_h)
        for j in range(2):
            extra = sign_ref[...] * edge_out[pl.ds(c0 + j, 1), :]
            out_ref[pl.ds(c0 + j, COARSE, stride=OWN), :] = (
                result[:, j * LANES:(j + 1) * LANES] + extra
            )
        return carry

    lax.fori_loop(0, OWN // 2, pair, 0)


def convolve(x):
    consts = [jnp.asarray(t) for t in tables()]
    return pl.pallas_call(
        convolve_kernel,
        out_shape=jax.ShapeDtypeStruct((COARSE * OWN, LANES), jnp.float32),
        scratch_shapes=[pltpu.VMEM((OWN, LANES), jnp.float32)],
        compiler_params=pltpu.CompilerParams(vmem_limit_bytes=32 * 1024 * 1024),
        cost_estimate=pl.CostEstimate(flops=4 << 30, bytes_accessed=4 << 20, transcendentals=0),
    )(x, *consts)


def project_kernel(conv_ref, query_ref, w_ref, out_ref):
    conv = conv_ref[...].reshape(PEERS * OWN, LANES).T
    gated = (query_ref[...].astype(jnp.float32) * conv).astype(jnp.bfloat16)
    out_ref[...] = dot(gated, w_ref[...])


def project(conv, query, w_out):
    channels, width = w_out.shape
    return pl.pallas_call(
        project_kernel,
        grid=(SUB,),
        in_specs=[
            pl.BlockSpec((PEERS, OWN, LANES), lambda e: (0, e, 0)),
            pl.BlockSpec((LANES, channels), lambda e: (e, 0)),
            pl.BlockSpec((channels, width), lambda e: (0, 0)),
        ],
        out_specs=pl.BlockSpec((LANES, width), lambda e: (e, 0)),
        out_shape=jax.ShapeDtypeStruct((SUB * LANES, width), jnp.float32),
        compiler_params=pltpu.CompilerParams(vmem_limit_bytes=40 * 1024 * 1024),
        cost_estimate=pl.CostEstimate(flops=2 << 30, bytes_accessed=14 << 20, transcendentals=0),
    )(conv, query, w_out)


def shards(query, key_stream, value, long_filter, w_out):
    sent = prepare(key_stream, value, long_filter)
    moved = lax.all_to_all(sent, "seq", split_axis=0, concat_axis=0, tiled=True)
    conv = convolve(moved.reshape(PEERS * 2 * SUB * OWN, LANES))
    home = lax.all_to_all(
        conv.reshape(PEERS, SUB * OWN, LANES), "seq", split_axis=0, concat_axis=0, tiled=True
    )
    partial_sums = project(home, query, w_out)
    return lax.psum_scatter(partial_sums, "chan", scatter_dimension=1, tiled=True).astype(
        jnp.bfloat16
    )


def solution(mesh):
    in_specs = (
        P("seq", "chan"),
        P("seq", "chan"),
        P("seq", "chan"),
        P("seq", "chan"),
        P("chan", None),
    )
    out_specs = P("seq", "chan")
    return jax.shard_map(shards, mesh=mesh, in_specs=in_specs, out_specs=out_specs, check_vma=False)
```

```python
import jax
import jax.numpy as jnp
import numpy as np
from jax import lax
from jax.experimental import pallas as pl
from jax.experimental.pallas import tpu as pltpu
from jax.sharding import PartitionSpec as P

LANES = 128
COARSE = 128
TOTAL = 2 * COARSE * LANES
PEERS = 32
OWN = 16
SUB = 4
CHIPS = 4
BLOCK = 512
GROUP = 8
BIG = 56 * 1024 * 1024
SMALL = 24 * 1024 * 1024


def split_bf16(x):
    high = x.astype(jnp.bfloat16)
    low = (x - high.astype(jnp.float32)).astype(jnp.bfloat16)
    return high, low


def tables():
    k = np.arange(COARSE)
    q = np.arange(COARSE)
    r = np.arange(LANES)
    coarse = 2.0 * np.pi * ((k[:, None] * q[None, :]) % (2 * COARSE)) / (2 * COARSE)
    first = np.concatenate([np.cos(coarse), -np.sin(coarse)], 0)
    fine = 2.0 * np.pi * ((r[:, None] * r[None, :]) % LANES) / LANES
    cos_f, sin_f = np.cos(fine), np.sin(fine)
    second = np.block([[cos_f, -sin_f], [sin_f, cos_f]])
    second_inv = np.block([[cos_f, sin_f], [-sin_f, cos_f]])
    weight = np.where(k == 0, 1.0, 2.0)[None, :] / TOTAL
    last = np.concatenate([weight * np.cos(coarse.T), -weight * np.sin(coarse.T)], 1)
    twist = 2.0 * np.pi * ((k[:, None] * r[None, :]) % TOTAL) / TOTAL
    middle = 2.0 * np.pi * (COARSE * r) / TOTAL
    edge = np.stack([np.cos(middle), np.sin(middle)], 0)
    sign = np.broadcast_to(np.where(q % 2 == 0, 1.0, -1.0)[:, None] / TOTAL, (COARSE, LANES))
    f32 = lambda x: np.ascontiguousarray(x).astype(np.float32)
    return [f32(t) for t in (first, second, second_inv, last, np.cos(twist), np.sin(twist), edge, sign)]


def prepare_kernel(key_ref, value_ref, taps_ref, out_ref):
    signal = key_ref[...].astype(jnp.float32) * value_ref[...].astype(jnp.float32)
    taps = taps_ref[...]
    for e in range(signal.shape[0] // LANES):
        rows = slice(e * LANES, (e + 1) * LANES)
        for s, stream in enumerate((signal, taps)):
            at = (2 * e + s) * OWN
            out_ref[:, at:at + OWN, :] = stream[rows, :].T.reshape(PEERS, OWN, LANES)


def prepare(key_stream, value, taps):
    rows, channels = key_stream.shape
    steps = 2
    block = pl.BlockSpec((rows // steps, channels), lambda i: (i, 0))
    sent = 2 * SUB * OWN
    return pl.pallas_call(
        prepare_kernel,
        grid=(steps,),
        in_specs=[block, block, block],
        out_specs=pl.BlockSpec((PEERS, sent // steps, LANES), lambda i: (0, i, 0)),
        out_shape=jax.ShapeDtypeStruct((PEERS, sent, LANES), jnp.float32),
        compiler_params=pltpu.CompilerParams(vmem_limit_bytes=BIG),
        cost_estimate=pl.CostEstimate(flops=0, bytes_accessed=4 << 20, transcendentals=0),
    )(key_stream, value, taps)


def dot(a, b):
    return jnp.dot(a, b, preferred_element_type=jnp.float32)


def rows_by(a, stacked):
    high, low = split_bf16(a)
    return dot(jnp.concatenate([high, low, high], 1), stacked)


def by_columns(stacked, a):
    high, low = split_bf16(a)
    return dot(stacked, jnp.concatenate([high, low, high], 0))


def multiply(a, b):
    ar, ai, br, bi = a[:, :LANES], a[:, LANES:], b[:, :LANES], b[:, LANES:]
    return jnp.concatenate([ar * br - ai * bi, ar * bi + ai * br], 1)


def convolve_kernel(
    x_ref, first_ref, second_ref, inverse_ref, last_ref, cos_ref, sin_ref, edge_ref, sign_ref,
    out_ref, edge_out, first, second, inverse, last,
):
    for ref, table, axis in (
        (first_ref, first, 1), (second_ref, second, 0), (inverse_ref, inverse, 0), (last_ref, last, 1)
    ):
        high, low = split_bf16(ref[...])
        table[...] = jnp.concatenate([high, high, low], axis)

    def add_pair(i, total):
        at = pl.multiple_of(i * (4 * OWN), 4 * OWN)
        return total + (x_ref[pl.ds(at, 2 * OWN), :] - x_ref[pl.ds(at + 2 * OWN, 2 * OWN), :])

    half = lax.fori_loop(
        0, COARSE // 2, add_pair, jnp.zeros((2 * OWN, LANES), jnp.float32), unroll=8
    )
    edge_cos, edge_sin = edge_ref[0:1, :], edge_ref[1:2, :]
    spectrum = rows_by(jnp.concatenate([half * edge_cos, -half * edge_sin], 1), second[...])
    back = rows_by(multiply(spectrum[:OWN], spectrum[OWN:]), inverse[...])
    edge_out[...] = back[:, :LANES] * edge_cos - back[:, LANES:] * edge_sin

    def some_channels(i, carry):
        c0 = GROUP * i
        streams = [
            x_ref[pl.ds(s * OWN + c0 + j, COARSE, stride=2 * OWN), :]
            for j in range(GROUP) for s in range(2)
        ]
        y = by_columns(first[...], jnp.concatenate(streams, 1))
        cos, sin = cos_ref[...], sin_ref[...]
        turned = []
        for j in range(2 * GROUP):
            yr = y[:COARSE, j * LANES:(j + 1) * LANES]
            yi = y[COARSE:, j * LANES:(j + 1) * LANES]
            turned.append(jnp.concatenate([yr * cos + yi * sin, yi * cos - yr * sin], 1))
        z = rows_by(jnp.concatenate(turned, 0), second[...])
        products = [
            multiply(
                z[2 * j * COARSE:(2 * j + 1) * COARSE], z[(2 * j + 1) * COARSE:(2 * j + 2) * COARSE]
            )
            for j in range(GROUP)
        ]
        u = rows_by(jnp.concatenate(products, 0), inverse[...])
        columns = []
        for j in range(GROUP):
            ur = u[j * COARSE:(j + 1) * COARSE, :LANES]
            ui = u[j * COARSE:(j + 1) * COARSE, LANES:]
            columns.append(jnp.concatenate([ur * cos - ui * sin, ur * sin + ui * cos], 0))
        result = by_columns(last[...], jnp.concatenate(columns, 1))
        for j in range(GROUP):
            extra = sign_ref[...] * edge_out[pl.ds(c0 + j, 1), :]
            out_ref[pl.ds(c0 + j, COARSE, stride=OWN), :] = (
                result[:, j * LANES:(j + 1) * LANES] + extra
            )
        return carry

    lax.fori_loop(0, OWN // GROUP, some_channels, 0)


def convolve(x):
    consts = [jnp.asarray(t) for t in tables()]
    return pl.pallas_call(
        convolve_kernel,
        out_shape=jax.ShapeDtypeStruct((COARSE * OWN, LANES), jnp.float32),
        scratch_shapes=[
            pltpu.VMEM((OWN, LANES), jnp.float32),
            pltpu.VMEM((2 * COARSE, 3 * COARSE), jnp.bfloat16),
            pltpu.VMEM((6 * LANES, 2 * LANES), jnp.bfloat16),
            pltpu.VMEM((6 * LANES, 2 * LANES), jnp.bfloat16),
            pltpu.VMEM((COARSE, 6 * COARSE), jnp.bfloat16),
        ],
        compiler_params=pltpu.CompilerParams(vmem_limit_bytes=SMALL),
        cost_estimate=pl.CostEstimate(flops=4 << 30, bytes_accessed=4 << 20, transcendentals=0),
    )(x, *consts)


def widen_kernel(where_ref, both_ref, first_ref, second_ref, one_ref, two_ref):
    both = both_ref[...].astype(jnp.float32)
    one_ref[0], one_ref[1] = both, first_ref[...].astype(jnp.float32)
    two_ref[0], two_ref[1] = both, second_ref[...].astype(jnp.float32)


def widen(w_out, where):
    channels, width = w_out.shape
    quarter = width // CHIPS
    steps = 2
    rows = channels // steps
    column = lambda n: pl.BlockSpec((rows, quarter), lambda i, where: (i, where[n]))
    out = pl.BlockSpec((2, rows, quarter), lambda i, where: (0, i, 0))
    shape = jax.ShapeDtypeStruct((2, channels, quarter), jnp.float32)
    return pl.pallas_call(
        widen_kernel,
        grid_spec=pltpu.PrefetchScalarGridSpec(
            num_scalar_prefetch=1,
            grid=(steps,),
            in_specs=[column(0), column(1), column(2)],
            out_specs=(out, out),
        ),
        out_shape=(shape, shape),
        compiler_params=pltpu.CompilerParams(vmem_limit_bytes=BIG),
        cost_estimate=pl.CostEstimate(flops=0, bytes_accessed=11 << 20, transcendentals=0),
    )(where, w_out, w_out, w_out)


def gate_kernel(conv_ref, query_ref, top_ref, bottom_ref):
    for e in range(SUB):
        rows = slice(e * LANES, (e + 1) * LANES)
        conv = conv_ref[:, e * OWN:(e + 1) * OWN, :].reshape(PEERS * OWN, LANES).T
        gated = query_ref[rows, :].astype(jnp.float32) * conv
        out_ref = top_ref if e < SUB // 2 else bottom_ref
        at = (e % (SUB // 2)) * LANES
        out_ref[at:at + LANES, :] = gated.astype(jnp.bfloat16).astype(jnp.float32)


def gate(conv, query):
    rows, channels = query.shape
    half = jax.ShapeDtypeStruct((rows // 2, channels), jnp.float32)
    return pl.pallas_call(
        gate_kernel,
        out_shape=(half, half),
        compiler_params=pltpu.CompilerParams(vmem_limit_bytes=SMALL),
        cost_estimate=pl.CostEstimate(flops=0, bytes_accessed=3 << 20, transcendentals=0),
    )(conv, query)


def own_kernel(where_ref, top_ref, bottom_ref, w_ref, out_ref):
    gated = jnp.where(pl.program_id(0) % 2 == 0, top_ref[...], bottom_ref[...])
    out_ref[...] = dot(gated.astype(jnp.bfloat16), w_ref[...])


def own_part(top, bottom, w_out, where):
    rows, channels = top.shape
    quarter = w_out.shape[1] // CHIPS
    whole = pl.BlockSpec((rows, channels), lambda i, where: (0, 0))
    return pl.pallas_call(
        own_kernel,
        grid_spec=pltpu.PrefetchScalarGridSpec(
            num_scalar_prefetch=1,
            grid=(4,),
            in_specs=[whole, whole, pl.BlockSpec((channels, quarter), lambda i, where: (0, where[i]))],
            out_specs=pl.BlockSpec((None, None, rows, quarter), lambda i, where: (i // 2, i % 2, 0, 0)),
        ),
        out_shape=jax.ShapeDtypeStruct((2, 2, rows, quarter), jnp.float32),
        compiler_params=pltpu.CompilerParams(vmem_limit_bytes=SMALL),
        cost_estimate=pl.CostEstimate(flops=1 << 30, bytes_accessed=8 << 20, transcendentals=0),
    )(where, top, bottom, w_out)


def add_kernel(core_ref, acc_ref, top_ref, bottom_ref, w_top_ref, w_bottom_ref, out_ref):
    for i, (gated, w) in enumerate(((top_ref, w_top_ref), (bottom_ref, w_bottom_ref))):
        out_ref[i] = acc_ref[i] + dot(
            gated[...].astype(jnp.bfloat16), w[...].astype(jnp.bfloat16)
        )


def add_partner(acc, top, bottom, w_top, w_bottom, which, parity):
    rows, channels = top.shape
    steps = 2
    columns = BLOCK // steps
    at = lambda n, parity: parity[0] * steps + n
    whole = pl.BlockSpec((rows, channels), lambda n, parity: (0, 0))
    weights = pl.BlockSpec((None, channels, columns), lambda n, parity: (which, 0, at(n, parity)))
    return pl.pallas_call(
        add_kernel,
        grid_spec=pltpu.PrefetchScalarGridSpec(
            num_scalar_prefetch=1,
            grid=(steps,),
            in_specs=[
                pl.BlockSpec(
                    (None, 2, rows, columns), lambda n, parity: (which, 0, 0, at(n, parity))
                ),
                whole,
                whole,
                weights,
                weights,
            ],
            out_specs=pl.BlockSpec((2, rows, columns), lambda n, parity: (0, 0, n)),
        ),
        out_shape=jax.ShapeDtypeStruct((2, rows, BLOCK), jnp.float32),
        compiler_params=pltpu.CompilerParams(vmem_limit_bytes=SMALL),
        cost_estimate=pl.CostEstimate(flops=1 << 28, bytes_accessed=5 << 20, transcendentals=0),
    )(parity, acc, top, bottom, w_top, w_bottom)


def sum_kernel(a_ref, b_ref, top_ref, bottom_ref):
    top_ref[...] = a_ref[0] + b_ref[0]
    bottom_ref[...] = a_ref[1] + b_ref[1]


def sum_cores(a, b):
    half = jax.ShapeDtypeStruct(a.shape[1:], jnp.float32)
    return pl.pallas_call(
        sum_kernel,
        out_shape=(half, half),
        compiler_params=pltpu.CompilerParams(vmem_limit_bytes=SMALL),
        cost_estimate=pl.CostEstimate(flops=1 << 18, bytes_accessed=3 << 20, transcendentals=0),
    )(a, b)


def last_kernel(a_ref, b_ref, top_ref, bottom_ref, out_ref):
    rows = top_ref.shape[0]
    for i, far in enumerate((top_ref, bottom_ref)):
        total = a_ref[i] + b_ref[i] + far[...]
        out_ref[i * rows:(i + 1) * rows, :] = total.astype(out_ref.dtype)


def last_sum(a, b, top, bottom):
    rows, columns = top.shape
    return pl.pallas_call(
        last_kernel,
        out_shape=jax.ShapeDtypeStruct((2 * rows, columns), jnp.bfloat16),
        compiler_params=pltpu.CompilerParams(vmem_limit_bytes=SMALL),
        cost_estimate=pl.CostEstimate(flops=1 << 19, bytes_accessed=4 << 20, transcendentals=0),
    )(a, b, top, bottom)


def shards(query, key_stream, value, long_filter, w_out):
    index = lax.axis_index("chan")
    chip, core = index // 2, index % 2
    step = 1 - 2 * (chip % 2)
    one, two, opposite = (chip + step) % CHIPS, (chip - step) % CHIPS, (chip + 2) % CHIPS
    size = 2 * CHIPS
    send_one = lambda x: lax.ppermute(x, "chan", [(i, i ^ 2) for i in range(size)])
    send_two = lambda x: lax.ppermute(
        x, "chan", [(i, (i - 2 if i // 2 % 2 == 0 else i + 2) % size) for i in range(size)]
    )
    send_core = lambda x: lax.ppermute(x, "chan", [(i, i ^ 1) for i in range(size)])

    sent = prepare(key_stream, value, long_filter)
    wide_one, wide_two = widen(w_out, jnp.stack([opposite, one, two]))
    w_one, w_two = send_one(wide_one), send_two(wide_two)
    moved = lax.all_to_all(sent, "seq", split_axis=0, concat_axis=0, tiled=True)
    conv = convolve(moved.reshape(PEERS * 2 * SUB * OWN, LANES))
    home = lax.all_to_all(
        conv.reshape(PEERS, SUB * OWN, LANES), "seq", split_axis=0, concat_axis=0, tiled=True
    )
    top, bottom = gate(home, query)
    top_one, bottom_two = send_one(top), send_two(bottom)
    acc = own_part(top, bottom, w_out, jnp.stack([two, one, chip, chip]))
    mine, theirs = core.reshape(1), (1 - core).reshape(1)
    add = lambda which, parity: add_partner(
        acc, top_one, bottom_two, w_one, w_two, which, parity
    )
    away_top, away_bottom = sum_cores(add(0, mine), send_core(add(0, theirs)))
    from_two, from_one = send_two(away_top), send_one(away_bottom)
    return last_sum(add(1, mine), send_core(add(1, theirs)), from_two, from_one)


def solution(mesh):
    in_specs = (
        P("seq", "chan"),
        P("seq", "chan"),
        P("seq", "chan"),
        P("seq", "chan"),
        P("chan", None),
    )
    out_specs = P("seq", "chan")
    return jax.shard_map(shards, mesh=mesh, in_specs=in_specs, out_specs=out_specs, check_vma=False)
```

```python
import functools

import jax
import jax.numpy as jnp
import numpy as np
from jax import lax
from jax.experimental import pallas as pl
from jax.experimental.pallas import tpu as pltpu
from jax.sharding import PartitionSpec as P

LANES = 128
COARSE = 128
TOTAL = 2 * COARSE * LANES
PEERS = 32
OWN = 16
SUB = 4
CHIPS = 4
BLOCK = 512
MAIN = 416
TAIL = 48
GROUP = 8
BIG = 56 * 1024 * 1024
SMALL = 24 * 1024 * 1024


def split_bf16(x):
    high = x.astype(jnp.bfloat16)
    low = (x - high.astype(jnp.float32)).astype(jnp.bfloat16)
    return high, low


def tables():
    k = np.arange(COARSE)
    q = np.arange(COARSE)
    r = np.arange(LANES)
    coarse = 2.0 * np.pi * ((k[:, None] * q[None, :]) % (2 * COARSE)) / (2 * COARSE)
    first = np.concatenate([np.cos(coarse), -np.sin(coarse)], 0)
    fine = 2.0 * np.pi * ((r[:, None] * r[None, :]) % LANES) / LANES
    cos_f, sin_f = np.cos(fine), np.sin(fine)
    second = np.block([[cos_f, -sin_f], [sin_f, cos_f]])
    second_inv = np.block([[cos_f, sin_f], [-sin_f, cos_f]])
    weight = np.where(k == 0, 1.0, 2.0)[None, :] / TOTAL
    last = np.concatenate([weight * np.cos(coarse.T), -weight * np.sin(coarse.T)], 1)
    twist = 2.0 * np.pi * ((k[:, None] * r[None, :]) % TOTAL) / TOTAL
    middle = 2.0 * np.pi * (COARSE * r) / TOTAL
    edge = np.tile(np.concatenate([np.cos(middle), np.sin(middle)])[None, :], (8, 1))
    rows = [
        np.concatenate([first[:COARSE], first[COARSE:]], 1), second, second_inv, last,
        np.concatenate([np.cos(twist), np.sin(twist)], 1), edge,
    ]
    return np.concatenate(rows, 0).astype(np.float32)


def prepare_kernel(key_ref, value_ref, taps_ref, out_ref):
    signal = key_ref[...].astype(jnp.float32) * value_ref[...].astype(jnp.float32)
    taps = taps_ref[...]
    for e in range(signal.shape[0] // LANES):
        rows = slice(e * LANES, (e + 1) * LANES)
        for s, stream in enumerate((signal, taps)):
            at = (2 * e + s) * OWN
            out_ref[:, at:at + OWN, :] = stream[rows, :].T.reshape(PEERS, OWN, LANES)


def prepare(key_stream, value, taps):
    rows, channels = key_stream.shape
    steps = 2
    block = pl.BlockSpec((rows // steps, channels), lambda i: (i, 0))
    sent = 2 * SUB * OWN
    return pl.pallas_call(
        prepare_kernel,
        grid=(steps,),
        in_specs=[block, block, block],
        out_specs=pl.BlockSpec((PEERS, sent // steps, LANES), lambda i: (0, i, 0)),
        out_shape=jax.ShapeDtypeStruct((PEERS, sent, LANES), jnp.float32),
        compiler_params=pltpu.CompilerParams(vmem_limit_bytes=BIG),
        cost_estimate=pl.CostEstimate(flops=0, bytes_accessed=4 << 20, transcendentals=0),
    )(key_stream, value, taps)


def dot(a, b):
    return jnp.dot(a, b, preferred_element_type=jnp.float32)


def rows_by(a, stacked):
    high, low = split_bf16(a)
    return dot(jnp.concatenate([high, low, high], 1), stacked)


def by_columns(stacked, a):
    high, low = split_bf16(a)
    return dot(stacked, jnp.concatenate([high, low, high], 0))


def multiply(a, b):
    ar, ai, br, bi = a[:, :LANES], a[:, LANES:], b[:, :LANES], b[:, LANES:]
    return jnp.concatenate([ar * br - ai * bi, ar * bi + ai * br], 1)


def convolve_kernel(
    x_ref, table_ref, one_ref, two_ref, out_ref, edge_out, first, second, inverse, last,
):
    ends = np.cumsum([0, COARSE, 2 * LANES, 2 * LANES, COARSE, COARSE, 8])
    first_at, second_at, inverse_at, last_at, twist_at, edge_at = [
        slice(int(p), int(q)) for p, q in zip(ends[:-1], ends[1:])
    ]
    re_im = table_ref[first_at, :]
    for values, table, axis in (
        (jnp.concatenate([re_im[:, :COARSE], re_im[:, COARSE:]], 0), first, 1),
        (table_ref[second_at, :], second, 0),
        (table_ref[inverse_at, :], inverse, 0),
        (table_ref[last_at, :], last, 1),
    ):
        high, low = split_bf16(values)
        table[...] = jnp.concatenate([high, high, low], axis)
    odd = lax.broadcasted_iota(jnp.int32, (COARSE, LANES), 0) % 2
    sign = jnp.where(odd == 0, 1.0 / TOTAL, -1.0 / TOTAL)
    edge = table_ref[edge_at, :][:1]

    def add_pair(i, total):
        at = pl.multiple_of(i * (4 * OWN), 4 * OWN)
        return total + (x_ref[pl.ds(at, 2 * OWN), :] - x_ref[pl.ds(at + 2 * OWN, 2 * OWN), :])

    half = lax.fori_loop(
        0, COARSE // 2, add_pair, jnp.zeros((2 * OWN, LANES), jnp.float32), unroll=8
    )
    edge_cos, edge_sin = edge[:, :LANES], edge[:, LANES:]
    spectrum = rows_by(jnp.concatenate([half * edge_cos, -half * edge_sin], 1), second[...])
    back = rows_by(multiply(spectrum[:OWN], spectrum[OWN:]), inverse[...])
    edge_out[...] = back[:, :LANES] * edge_cos - back[:, LANES:] * edge_sin

    def some_channels(i, carry):
        c0 = GROUP * i
        streams = [
            x_ref[pl.ds(s * OWN + c0 + j, COARSE, stride=2 * OWN), :]
            for j in range(GROUP) for s in range(2)
        ]
        y = by_columns(first[...], jnp.concatenate(streams, 1))
        cos, sin = table_ref[twist_at, :LANES], table_ref[twist_at, LANES:]
        turned = []
        for j in range(2 * GROUP):
            yr = y[:COARSE, j * LANES:(j + 1) * LANES]
            yi = y[COARSE:, j * LANES:(j + 1) * LANES]
            turned.append(jnp.concatenate([yr * cos + yi * sin, yi * cos - yr * sin], 1))
        z = rows_by(jnp.concatenate(turned, 0), second[...])
        products = [
            multiply(
                z[2 * j * COARSE:(2 * j + 1) * COARSE], z[(2 * j + 1) * COARSE:(2 * j + 2) * COARSE]
            )
            for j in range(GROUP)
        ]
        u = rows_by(jnp.concatenate(products, 0), inverse[...])
        columns = []
        for j in range(GROUP):
            ur = u[j * COARSE:(j + 1) * COARSE, :LANES]
            ui = u[j * COARSE:(j + 1) * COARSE, LANES:]
            columns.append(jnp.concatenate([ur * cos - ui * sin, ur * sin + ui * cos], 0))
        result = by_columns(last[...], jnp.concatenate(columns, 1))
        for j in range(GROUP):
            extra = sign * edge_out[pl.ds(c0 + j, 1), :]
            out_ref[pl.ds(c0 + j, COARSE, stride=OWN), :] = (
                result[:, j * LANES:(j + 1) * LANES] + extra
            )
        return carry

    lax.fori_loop(0, OWN // GROUP, some_channels, 0)


def convolve(x, *before):
    return pl.pallas_call(
        convolve_kernel,
        in_specs=[pl.BlockSpec()] * 2 + [pl.BlockSpec(memory_space=pltpu.VMEM)] * 2,
        out_shape=jax.ShapeDtypeStruct((COARSE * OWN, LANES), jnp.float32),
        scratch_shapes=[
            pltpu.VMEM((OWN, LANES), jnp.float32),
            pltpu.VMEM((2 * COARSE, 3 * COARSE), jnp.bfloat16),
            pltpu.VMEM((6 * LANES, 2 * LANES), jnp.bfloat16),
            pltpu.VMEM((6 * LANES, 2 * LANES), jnp.bfloat16),
            pltpu.VMEM((COARSE, 6 * COARSE), jnp.bfloat16),
        ],
        compiler_params=pltpu.CompilerParams(vmem_limit_bytes=SMALL),
        cost_estimate=pl.CostEstimate(flops=4 << 30, bytes_accessed=4 << 20, transcendentals=0),
    )(x, jnp.asarray(tables()), *before)


def widen_kernel(where_ref, w_ref, one_tail, two_tail, one_main, two_main):
    quarter = one_main.shape[2]
    main = pl.ds(0, MAIN)
    tail = pl.ds(pl.multiple_of(MAIN + where_ref[3] * TAIL, 16), TAIL)
    for rows, one_ref, two_ref in ((tail, one_tail, two_tail), (main, one_main, two_main)):
        for n, refs in enumerate(((one_ref.at[0], two_ref.at[0]), (one_ref.at[1],), (two_ref.at[1],))):
            at = pl.ds(pl.multiple_of(where_ref[n] * quarter, quarter), quarter)
            wide = w_ref[rows, at].astype(jnp.float32)
            for ref in refs:
                ref[...] = wide


def widen(w_out, where):
    quarter = w_out.shape[1] // CHIPS
    tail = jax.ShapeDtypeStruct((2, TAIL, quarter), jnp.float32)
    main = jax.ShapeDtypeStruct((2, MAIN, quarter), jnp.float32)
    in_vmem = pl.BlockSpec(memory_space=pltpu.VMEM)
    return pl.pallas_call(
        widen_kernel,
        in_specs=[pl.BlockSpec(memory_space=pltpu.SMEM), in_vmem],
        out_specs=(in_vmem,) * 4,
        out_shape=(tail, tail, main, main),
        compiler_params=pltpu.CompilerParams(vmem_limit_bytes=SMALL),
        cost_estimate=pl.CostEstimate(flops=0, bytes_accessed=11 << 20, transcendentals=0),
    )(where, w_out)


def narrow_kernel(mine_ref, one_main, two_main, one_tail, two_tail, one_far, two_far, one_out, two_out):
    mine = pl.ds(pl.multiple_of(MAIN + mine_ref[0] * TAIL, 16), TAIL)
    theirs = pl.ds(pl.multiple_of(MAIN + (1 - mine_ref[0]) * TAIL, 16), TAIL)
    for main, tail, far, out in (
        (one_main, one_tail, one_far, one_out), (two_main, two_tail, two_far, two_out)
    ):
        out[:MAIN, :] = main[...].astype(jnp.bfloat16)
        out[mine, :] = tail[...].astype(jnp.bfloat16)
        out[theirs, :] = far[...].astype(jnp.bfloat16)


def narrow(mine, *parts):
    quarter = parts[0].shape[2]
    block = lambda rows: pl.BlockSpec((None, rows, quarter), lambda i, mine: (i, 0, 0))
    channels = MAIN + 2 * TAIL
    shape = jax.ShapeDtypeStruct((2, channels, quarter), jnp.bfloat16)
    return pl.pallas_call(
        narrow_kernel,
        grid_spec=pltpu.PrefetchScalarGridSpec(
            num_scalar_prefetch=1,
            grid=(2,),
            in_specs=[block(MAIN)] * 2 + [block(TAIL)] * 4,
            out_specs=(block(channels), block(channels)),
        ),
        out_shape=(shape, shape),
        compiler_params=pltpu.CompilerParams(vmem_limit_bytes=SMALL),
        cost_estimate=pl.CostEstimate(flops=0, bytes_accessed=12 << 20, transcendentals=0),
    )(mine, *parts)


def gate_kernel(conv_ref, query_ref, top_ref, bottom_ref):
    for e in range(SUB):
        rows = slice(e * LANES, (e + 1) * LANES)
        conv = conv_ref[:, e * OWN:(e + 1) * OWN, :].reshape(PEERS * OWN, LANES).T
        gated = query_ref[rows, :].astype(jnp.float32) * conv
        out_ref = top_ref if e < SUB // 2 else bottom_ref
        at = (e % (SUB // 2)) * LANES
        out_ref[at:at + LANES, :] = gated.astype(jnp.bfloat16).astype(jnp.float32)


def gate(conv, query):
    rows, channels = query.shape
    half = jax.ShapeDtypeStruct((rows // 2, channels), jnp.float32)
    return pl.pallas_call(
        gate_kernel,
        out_shape=(half, half),
        compiler_params=pltpu.CompilerParams(vmem_limit_bytes=SMALL),
        cost_estimate=pl.CostEstimate(flops=0, bytes_accessed=3 << 20, transcendentals=0),
    )(conv, query)


def own_kernel(where_ref, top_ref, bottom_ref, w_ref, out_ref):
    gated = jnp.where(pl.program_id(0) % 2 == 0, top_ref[...], bottom_ref[...])
    out_ref[...] = dot(gated.astype(jnp.bfloat16), w_ref[...])


def own_part(top, bottom, w_out, where):
    rows, channels = top.shape
    quarter = w_out.shape[1] // CHIPS
    whole = pl.BlockSpec((rows, channels), lambda i, where: (0, 0))
    return pl.pallas_call(
        own_kernel,
        grid_spec=pltpu.PrefetchScalarGridSpec(
            num_scalar_prefetch=1,
            grid=(4,),
            in_specs=[whole, whole, pl.BlockSpec((channels, quarter), lambda i, where: (0, where[i]))],
            out_specs=pl.BlockSpec((None, None, rows, quarter), lambda i, where: (i // 2, i % 2, 0, 0)),
        ),
        out_shape=jax.ShapeDtypeStruct((2, 2, rows, quarter), jnp.float32),
        compiler_params=pltpu.CompilerParams(vmem_limit_bytes=SMALL),
        cost_estimate=pl.CostEstimate(flops=1 << 30, bytes_accessed=8 << 20, transcendentals=0),
    )(where, top, bottom, w_out)


def add_kernel(jobs, core_ref, acc_ref, top_ref, bottom_ref, w_top_ref, w_bottom_ref, *out_refs):
    for (which, own), out_ref in zip(jobs, out_refs):
        parity = core_ref[0] if own else 1 - core_ref[0]
        at = pl.ds(pl.multiple_of(parity * BLOCK, BLOCK), BLOCK)
        for i, (gated, w) in enumerate(((top_ref, w_top_ref), (bottom_ref, w_bottom_ref))):
            out_ref[i] = acc_ref[which, i, :, at] + dot(
                gated[...].astype(jnp.bfloat16), w[which, :, at]
            )


def add_partner(core, acc, top, bottom, w_top, w_bottom, jobs):
    rows = top.shape[0]
    shape = jax.ShapeDtypeStruct((2, rows, BLOCK), jnp.float32)
    return pl.pallas_call(
        functools.partial(add_kernel, jobs),
        in_specs=[pl.BlockSpec(memory_space=pltpu.SMEM)]
        + [pl.BlockSpec(memory_space=pltpu.VMEM)] * 5,
        out_specs=tuple(pl.BlockSpec(memory_space=pltpu.VMEM) for _ in jobs),
        out_shape=tuple(shape for _ in jobs),
        compiler_params=pltpu.CompilerParams(vmem_limit_bytes=SMALL),
        cost_estimate=pl.CostEstimate(
            flops=len(jobs) << 28, bytes_accessed=len(jobs) << 22, transcendentals=0
        ),
    )(core, acc, top, bottom, w_top, w_bottom)


def sum_kernel(a_ref, b_ref, top_ref, bottom_ref):
    top_ref[...] = a_ref[0] + b_ref[0]
    bottom_ref[...] = a_ref[1] + b_ref[1]


def sum_cores(a, b):
    half = jax.ShapeDtypeStruct(a.shape[1:], jnp.float32)
    return pl.pallas_call(
        sum_kernel,
        out_shape=(half, half),
        compiler_params=pltpu.CompilerParams(vmem_limit_bytes=SMALL),
        cost_estimate=pl.CostEstimate(flops=1 << 18, bytes_accessed=3 << 20, transcendentals=0),
    )(a, b)


def last_kernel(a_ref, b_ref, top_ref, bottom_ref, out_ref):
    rows = top_ref.shape[0]
    for i, far in enumerate((top_ref, bottom_ref)):
        total = a_ref[i] + b_ref[i] + far[...]
        out_ref[i * rows:(i + 1) * rows, :] = total.astype(out_ref.dtype)


def last_sum(a, b, top, bottom):
    rows, columns = top.shape
    return pl.pallas_call(
        last_kernel,
        out_shape=jax.ShapeDtypeStruct((2 * rows, columns), jnp.bfloat16),
        compiler_params=pltpu.CompilerParams(vmem_limit_bytes=SMALL),
        cost_estimate=pl.CostEstimate(flops=1 << 19, bytes_accessed=4 << 20, transcendentals=0),
    )(a, b, top, bottom)


def shards(query, key_stream, value, long_filter, w_out):
    index = lax.axis_index("chan")
    chip, core = index // 2, index % 2
    step = 1 - 2 * (chip % 2)
    one, two, opposite = (chip + step) % CHIPS, (chip - step) % CHIPS, (chip + 2) % CHIPS
    size = 2 * CHIPS
    send_one = lambda x: lax.ppermute(x, "chan", [(i, i ^ 2) for i in range(size)])
    send_two = lambda x: lax.ppermute(
        x, "chan", [(i, (i - 2 if i // 2 % 2 == 0 else i + 2) % size) for i in range(size)]
    )
    send_core = lambda x: lax.ppermute(x, "chan", [(i, i ^ 1) for i in range(size)])

    sent = prepare(key_stream, value, long_filter)
    side = lax.axis_index("seq") % 2
    send_side = lambda x: lax.ppermute(x, "seq", [(i, i ^ 1) for i in range(PEERS)])
    wide = widen(w_out, jnp.stack([opposite, one, two, side]))
    near_one, near_two = send_one(wide[0]), send_two(wide[1])
    main_one, main_two = send_one(wide[2]), send_two(wide[3])
    far_one, far_two = send_side(near_one), send_side(near_two)
    moved = lax.all_to_all(sent, "seq", split_axis=0, concat_axis=0, tiled=True)
    conv = convolve(moved.reshape(PEERS * 2 * SUB * OWN, LANES), far_one, far_two)
    home = lax.all_to_all(
        conv.reshape(PEERS, SUB * OWN, LANES), "seq", split_axis=0, concat_axis=0, tiled=True
    )
    top, bottom = gate(home, query)
    top_one, bottom_two = send_one(top), send_two(bottom)
    acc = own_part(top, bottom, w_out, jnp.stack([two, one, chip, chip]))
    narrow_one, narrow_two = narrow(
        side.reshape(1), main_one, main_two, near_one, near_two, far_one, far_two
    )
    add = lambda *jobs: add_partner(
        core.reshape(1), acc, top_one, bottom_two, narrow_one, narrow_two, jobs
    )
    other, own = 0, 1
    (away_sent,) = add((other, False))
    away_kept, here_sent = add((other, True), (own, False))
    away_top, away_bottom = sum_cores(away_kept, send_core(away_sent))
    from_two, from_one = send_two(away_top), send_one(away_bottom)
    (here_kept,) = add((own, True))
    return last_sum(here_kept, send_core(here_sent), from_two, from_one)


def solution(mesh):
    in_specs = (
        P("seq", "chan"),
        P("seq", "chan"),
        P("seq", "chan"),
        P("seq", "chan"),
        P("chan", None),
    )
    out_specs = P("seq", "chan")
    return jax.shard_map(shards, mesh=mesh, in_specs=in_specs, out_specs=out_specs, check_vma=False)
```

```python
import functools

import jax
import jax.numpy as jnp
import numpy as np
from jax import lax
from jax.experimental import pallas as pl
from jax.experimental.pallas import tpu as pltpu
from jax.sharding import PartitionSpec as P

LANES = 128
COARSE = 128
TOTAL = 2 * COARSE * LANES
PEERS = 32
OWN = 16
SUB = 4
CHIPS = 4
BLOCK = 512
MAIN = 448
TAIL = 32
GROUP = 16
BIG = 56 * 1024 * 1024
SMALL = 24 * 1024 * 1024


def split_bf16(x):
    high = x.astype(jnp.bfloat16)
    low = (x - high.astype(jnp.float32)).astype(jnp.bfloat16)
    return high, low


def tables():
    k = np.arange(COARSE)
    q = np.arange(COARSE)
    r = np.arange(LANES)
    coarse = 2.0 * np.pi * ((k[:, None] * q[None, :]) % (2 * COARSE)) / (2 * COARSE)
    fine = 2.0 * np.pi * ((r[:, None] * r[None, :]) % LANES) / LANES
    twist = 2.0 * np.pi * ((k[:, None] * r[None, :]) % TOTAL) / TOTAL
    middle = 2.0 * np.pi * np.tile((COARSE * r)[None, :], (8, 1)) / TOTAL
    rows = [
        np.concatenate([np.cos(angle), np.sin(angle)], 1) for angle in (coarse, fine, twist, middle)
    ]
    return np.concatenate(rows, 0).astype(np.float32)


def prepare_kernel(key_ref, value_ref, taps_ref, out_ref):
    signal = key_ref[...].astype(jnp.float32) * value_ref[...].astype(jnp.float32)
    taps = taps_ref[...]
    for e in range(signal.shape[0] // LANES):
        rows = slice(e * LANES, (e + 1) * LANES)
        for s, stream in enumerate((signal, taps)):
            at = (2 * e + s) * OWN
            out_ref[:, at:at + OWN, :] = stream[rows, :].T.reshape(PEERS, OWN, LANES)


def prepare(key_stream, value, taps):
    rows, channels = key_stream.shape
    steps = 2
    block = pl.BlockSpec((rows // steps, channels), lambda i: (i, 0))
    sent = 2 * SUB * OWN
    return pl.pallas_call(
        prepare_kernel,
        grid=(steps,),
        in_specs=[block, block, block],
        out_specs=pl.BlockSpec((PEERS, sent // steps, LANES), lambda i: (0, i, 0)),
        out_shape=jax.ShapeDtypeStruct((PEERS, sent, LANES), jnp.float32),
        compiler_params=pltpu.CompilerParams(vmem_limit_bytes=BIG),
        cost_estimate=pl.CostEstimate(flops=0, bytes_accessed=4 << 20, transcendentals=0),
    )(key_stream, value, taps)


def dot(a, b):
    return jnp.dot(a, b, preferred_element_type=jnp.float32)


def rows_by(a, stacked):
    high, low = split_bf16(a)
    return dot(jnp.concatenate([high, low, high], 1), stacked)


def by_columns(stacked, a):
    high, low = split_bf16(a)
    return dot(stacked, jnp.concatenate([high, low, high], 0))


def multiply(a, b):
    ar, ai, br, bi = a[:, :LANES], a[:, LANES:], b[:, :LANES], b[:, LANES:]
    return jnp.concatenate([ar * br - ai * bi, ar * bi + ai * br], 1)


def convolve_kernel(
    x_ref, table_ref, one_ref, two_ref, out_ref, edge_out, first, second, inverse, last,
):
    coarse_at, fine_at, twist_at = [slice(i * COARSE, (i + 1) * COARSE) for i in range(3)]
    edge_at = slice(3 * COARSE, 3 * COARSE + 1)
    cos, sin = table_ref[coarse_at, :LANES], table_ref[coarse_at, LANES:]
    lane = lax.broadcasted_iota(jnp.int32, (COARSE, COARSE), 1)
    weight = jnp.where(lane == 0, 1.0 / TOTAL, 2.0 / TOTAL)
    beside = lambda *parts: jnp.concatenate(parts, 1)
    over = lambda *parts: jnp.concatenate(parts, 0)
    fine_cos, fine_sin = table_ref[fine_at, :LANES], table_ref[fine_at, LANES:]
    for values, table, axis in (
        (over(cos, -sin), first, 1),
        (over(beside(fine_cos, -fine_sin), beside(fine_sin, fine_cos)), second, 0),
        (over(beside(fine_cos, fine_sin), beside(-fine_sin, fine_cos)), inverse, 0),
        (beside(weight * cos, -weight * sin), last, 1),
    ):
        high, low = split_bf16(values)
        table[...] = jnp.concatenate([high, high, low], axis)
    odd = lax.broadcasted_iota(jnp.int32, (COARSE, LANES), 0) % 2
    sign = jnp.where(odd == 0, 1.0 / TOTAL, -1.0 / TOTAL)
    edge = table_ref[edge_at, :]

    def add_pair(i, total):
        at = pl.multiple_of(i * (4 * OWN), 4 * OWN)
        return total + (x_ref[pl.ds(at, 2 * OWN), :] - x_ref[pl.ds(at + 2 * OWN, 2 * OWN), :])

    half = lax.fori_loop(
        0, COARSE // 2, add_pair, jnp.zeros((2 * OWN, LANES), jnp.float32), unroll=8
    )
    edge_cos, edge_sin = edge[:, :LANES], edge[:, LANES:]
    spectrum = rows_by(jnp.concatenate([half * edge_cos, -half * edge_sin], 1), second[...])
    back = rows_by(multiply(spectrum[:OWN], spectrum[OWN:]), inverse[...])
    edge_out[...] = back[:, :LANES] * edge_cos - back[:, LANES:] * edge_sin

    def some_channels(i, carry):
        c0 = GROUP * i
        streams = [
            x_ref[pl.ds(s * OWN + c0 + j, COARSE, stride=2 * OWN), :]
            for j in range(GROUP) for s in range(2)
        ]
        y = by_columns(first[...], jnp.concatenate(streams, 1))
        cos, sin = table_ref[twist_at, :LANES], table_ref[twist_at, LANES:]
        turned = []
        for j in range(2 * GROUP):
            yr = y[:COARSE, j * LANES:(j + 1) * LANES]
            yi = y[COARSE:, j * LANES:(j + 1) * LANES]
            turned.append(jnp.concatenate([yr * cos + yi * sin, yi * cos - yr * sin], 1))
        z = rows_by(jnp.concatenate(turned, 0), second[...])
        products = [
            multiply(
                z[2 * j * COARSE:(2 * j + 1) * COARSE], z[(2 * j + 1) * COARSE:(2 * j + 2) * COARSE]
            )
            for j in range(GROUP)
        ]
        u = rows_by(jnp.concatenate(products, 0), inverse[...])
        columns = []
        for j in range(GROUP):
            ur = u[j * COARSE:(j + 1) * COARSE, :LANES]
            ui = u[j * COARSE:(j + 1) * COARSE, LANES:]
            columns.append(jnp.concatenate([ur * cos - ui * sin, ur * sin + ui * cos], 0))
        result = by_columns(last[...], jnp.concatenate(columns, 1))
        for j in range(GROUP):
            extra = sign * edge_out[pl.ds(c0 + j, 1), :]
            out_ref[pl.ds(c0 + j, COARSE, stride=OWN), :] = (
                result[:, j * LANES:(j + 1) * LANES] + extra
            )
        return carry

    lax.fori_loop(0, OWN // GROUP, some_channels, 0)


def convolve(x, *before):
    return pl.pallas_call(
        convolve_kernel,
        in_specs=[pl.BlockSpec()] * 2 + [pl.BlockSpec(memory_space=pltpu.VMEM)] * 2,
        out_shape=jax.ShapeDtypeStruct((COARSE * OWN, LANES), jnp.float32),
        scratch_shapes=[
            pltpu.VMEM((OWN, LANES), jnp.float32),
            pltpu.VMEM((2 * COARSE, 3 * COARSE), jnp.bfloat16),
            pltpu.VMEM((6 * LANES, 2 * LANES), jnp.bfloat16),
            pltpu.VMEM((6 * LANES, 2 * LANES), jnp.bfloat16),
            pltpu.VMEM((COARSE, 6 * COARSE), jnp.bfloat16),
        ],
        compiler_params=pltpu.CompilerParams(vmem_limit_bytes=SMALL),
        cost_estimate=pl.CostEstimate(flops=4 << 30, bytes_accessed=4 << 20, transcendentals=0),
    )(x, jnp.asarray(tables()), *before)


def place():
    index = lax.axis_index("chan")
    chip, core = index // 2, index % 2
    step = 1 - 2 * (chip % 2)
    around = lambda n: (chip + CHIPS + n) % CHIPS
    return chip, core, around(step), around(-step), around(2)


def widen_kernel(tail, w_ref, one_ref, two_ref, buffer, arrived):
    rows, quarter = buffer.shape[1:]
    _, _, one, two, opposite = place()
    start = pl.multiple_of(MAIN + lax.axis_index("seq") % 2 * TAIL, 16) if tail else 0
    copies = []
    for n, column in enumerate((opposite, one, two)):
        at = pl.multiple_of(column * quarter, quarter)
        copies.append(
            pltpu.make_async_copy(
                w_ref.at[pl.ds(start, rows), pl.ds(at, quarter)], buffer.at[n], arrived.at[n]
            )
        )
        copies[n].start()
    for n, refs in enumerate(((one_ref.at[0], two_ref.at[0]), (one_ref.at[1],), (two_ref.at[1],))):
        copies[n].wait()
        wide = buffer[n].astype(jnp.float32)
        for ref in refs:
            ref[...] = wide


def widen(w_out, tail):
    rows = TAIL if tail else MAIN
    quarter = w_out.shape[1] // CHIPS
    shape = jax.ShapeDtypeStruct((2, rows, quarter), jnp.float32)
    return pl.pallas_call(
        functools.partial(widen_kernel, tail),
        in_specs=[pl.BlockSpec(memory_space=pltpu.HBM)],
        out_shape=(shape, shape),
        scratch_shapes=[
            pltpu.VMEM((3, rows, quarter), jnp.bfloat16),
            pltpu.SemaphoreType.DMA((3,)),
        ],
        compiler_params=pltpu.CompilerParams(vmem_limit_bytes=BIG),
        cost_estimate=pl.CostEstimate(
            flops=0, bytes_accessed=rows * quarter * 22, transcendentals=0
        ),
    )(w_out)


def after_kernel(x_ref, before_ref, out_ref):
    pass


def after(x, before):
    anywhere = pl.BlockSpec(memory_space=pl.ANY)
    return pl.pallas_call(
        after_kernel,
        in_specs=[anywhere, pl.BlockSpec(memory_space=pltpu.VMEM)],
        out_specs=anywhere,
        out_shape=jax.ShapeDtypeStruct(x.shape, x.dtype),
        input_output_aliases={0: 0},
        compiler_params=pltpu.CompilerParams(vmem_limit_bytes=SMALL),
        cost_estimate=pl.CostEstimate(flops=0, bytes_accessed=4096, transcendentals=0),
    )(x, before[0, :8, :LANES])


def narrow_kernel(mine_ref, one_main, two_main, one_tail, two_tail, one_far, two_far, one_out, two_out):
    mine = pl.ds(pl.multiple_of(MAIN + mine_ref[0] * TAIL, 16), TAIL)
    theirs = pl.ds(pl.multiple_of(MAIN + (1 - mine_ref[0]) * TAIL, 16), TAIL)
    for main, tail, far, out in (
        (one_main, one_tail, one_far, one_out), (two_main, two_tail, two_far, two_out)
    ):
        out[:MAIN, :] = main[...].astype(jnp.bfloat16)
        out[mine, :] = tail[...].astype(jnp.bfloat16)
        out[theirs, :] = far[...].astype(jnp.bfloat16)


def narrow(mine, *parts):
    quarter = parts[0].shape[2]
    block = lambda rows: pl.BlockSpec((None, rows, quarter), lambda i, mine: (i, 0, 0))
    channels = MAIN + 2 * TAIL
    shape = jax.ShapeDtypeStruct((2, channels, quarter), jnp.bfloat16)
    return pl.pallas_call(
        narrow_kernel,
        grid_spec=pltpu.PrefetchScalarGridSpec(
            num_scalar_prefetch=1,
            grid=(2,),
            in_specs=[block(MAIN)] * 2 + [block(TAIL)] * 4,
            out_specs=(block(channels), block(channels)),
        ),
        out_shape=(shape, shape),
        compiler_params=pltpu.CompilerParams(vmem_limit_bytes=SMALL),
        cost_estimate=pl.CostEstimate(flops=0, bytes_accessed=12 << 20, transcendentals=0),
    )(mine, *parts)


def gate_kernel(conv_ref, query_ref, top_ref, bottom_ref):
    for e in range(SUB):
        rows = slice(e * LANES, (e + 1) * LANES)
        conv = conv_ref[:, e * OWN:(e + 1) * OWN, :].reshape(PEERS * OWN, LANES).T
        gated = query_ref[rows, :].astype(jnp.float32) * conv
        out_ref = top_ref if e < SUB // 2 else bottom_ref
        at = (e % (SUB // 2)) * LANES
        out_ref[at:at + LANES, :] = gated.astype(jnp.bfloat16).astype(jnp.float32)


def gate(conv, query):
    rows, channels = query.shape
    half = jax.ShapeDtypeStruct((rows // 2, channels), jnp.float32)
    return pl.pallas_call(
        gate_kernel,
        out_shape=(half, half),
        compiler_params=pltpu.CompilerParams(vmem_limit_bytes=SMALL),
        cost_estimate=pl.CostEstimate(flops=0, bytes_accessed=3 << 20, transcendentals=0),
    )(conv, query)


def own_kernel(where_ref, top_ref, bottom_ref, w_ref, out_ref):
    gated = jnp.where(pl.program_id(0) % 2 == 0, top_ref[...], bottom_ref[...])
    out_ref[...] = dot(gated.astype(jnp.bfloat16), w_ref[...])


def own_part(top, bottom, w_out, where):
    rows, channels = top.shape
    quarter = w_out.shape[1] // CHIPS
    whole = pl.BlockSpec((rows, channels), lambda i, where: (0, 0))
    return pl.pallas_call(
        own_kernel,
        grid_spec=pltpu.PrefetchScalarGridSpec(
            num_scalar_prefetch=1,
            grid=(4,),
            in_specs=[whole, whole, pl.BlockSpec((channels, quarter), lambda i, where: (0, where[i]))],
            out_specs=pl.BlockSpec((None, None, rows, quarter), lambda i, where: (i // 2, i % 2, 0, 0)),
        ),
        out_shape=jax.ShapeDtypeStruct((2, 2, rows, quarter), jnp.float32),
        compiler_params=pltpu.CompilerParams(vmem_limit_bytes=SMALL),
        cost_estimate=pl.CostEstimate(flops=1 << 30, bytes_accessed=8 << 20, transcendentals=0),
    )(where, top, bottom, w_out)


def add_kernel(jobs, core_ref, acc_ref, top_ref, bottom_ref, w_top_ref, w_bottom_ref, *out_refs):
    for (which, own), out_ref in zip(jobs, out_refs):
        parity = core_ref[0] if own else 1 - core_ref[0]
        at = pl.ds(pl.multiple_of(parity * BLOCK, BLOCK), BLOCK)
        for i, (gated, w) in enumerate(((top_ref, w_top_ref), (bottom_ref, w_bottom_ref))):
            out_ref[i] = acc_ref[which, i, :, at] + dot(
                gated[...].astype(jnp.bfloat16), w[which, :, at]
            )


def add_partner(core, acc, top, bottom, w_top, w_bottom, jobs):
    rows = top.shape[0]
    shape = jax.ShapeDtypeStruct((2, rows, BLOCK), jnp.float32)
    return pl.pallas_call(
        functools.partial(add_kernel, jobs),
        in_specs=[pl.BlockSpec(memory_space=pltpu.SMEM)]
        + [pl.BlockSpec(memory_space=pltpu.VMEM)] * 5,
        out_specs=tuple(pl.BlockSpec(memory_space=pltpu.VMEM) for _ in jobs),
        out_shape=tuple(shape for _ in jobs),
        compiler_params=pltpu.CompilerParams(vmem_limit_bytes=SMALL),
        cost_estimate=pl.CostEstimate(
            flops=len(jobs) << 28, bytes_accessed=len(jobs) << 22, transcendentals=0
        ),
    )(core, acc, top, bottom, w_top, w_bottom)


def sum_kernel(a_ref, b_ref, top_ref, bottom_ref):
    top_ref[...] = a_ref[0] + b_ref[0]
    bottom_ref[...] = a_ref[1] + b_ref[1]


def sum_cores(a, b):
    half = jax.ShapeDtypeStruct(a.shape[1:], jnp.float32)
    return pl.pallas_call(
        sum_kernel,
        out_shape=(half, half),
        compiler_params=pltpu.CompilerParams(vmem_limit_bytes=SMALL),
        cost_estimate=pl.CostEstimate(flops=1 << 18, bytes_accessed=3 << 20, transcendentals=0),
    )(a, b)


def last_kernel(a_ref, b_ref, top_ref, bottom_ref, out_ref):
    rows = top_ref.shape[0]
    for i, far in enumerate((top_ref, bottom_ref)):
        total = a_ref[i] + b_ref[i] + far[...]
        out_ref[i * rows:(i + 1) * rows, :] = total.astype(out_ref.dtype)


def last_sum(a, b, top, bottom):
    rows, columns = top.shape
    return pl.pallas_call(
        last_kernel,
        out_shape=jax.ShapeDtypeStruct((2 * rows, columns), jnp.bfloat16),
        compiler_params=pltpu.CompilerParams(vmem_limit_bytes=SMALL),
        cost_estimate=pl.CostEstimate(flops=1 << 19, bytes_accessed=4 << 20, transcendentals=0),
    )(a, b, top, bottom)


def shards(query, key_stream, value, long_filter, w_out):
    chip, core, one, two, opposite = place()
    size = 2 * CHIPS
    send_one = lambda x: lax.ppermute(x, "chan", [(i, i ^ 2) for i in range(size)])
    send_two = lambda x: lax.ppermute(
        x, "chan", [(i, (i - 2 if i // 2 % 2 == 0 else i + 2) % size) for i in range(size)]
    )
    send_core = lambda x: lax.ppermute(x, "chan", [(i, i ^ 1) for i in range(size)])

    sent = prepare(key_stream, value, long_filter)
    side = lax.axis_index("seq") % 2
    send_side = lambda x: lax.ppermute(x, "seq", [(i, i ^ 1) for i in range(PEERS)])
    tail_one, tail_two = widen(w_out, True)
    near_one, near_two = send_one(tail_one), send_two(tail_two)
    wide_one, wide_two = widen(w_out, False)
    main_one, main_two = send_one(after(wide_one, near_one)), send_two(after(wide_two, near_two))
    far_one, far_two = send_side(near_one), send_side(near_two)
    moved = lax.all_to_all(sent, "seq", split_axis=0, concat_axis=0, tiled=True)
    conv = convolve(moved.reshape(PEERS * 2 * SUB * OWN, LANES), far_one[0, :8, :LANES], far_two[0, :8, :LANES])
    home = lax.all_to_all(
        conv.reshape(PEERS, SUB * OWN, LANES), "seq", split_axis=0, concat_axis=0, tiled=True
    )
    top, bottom = gate(home, query)
    top_one, bottom_two = send_one(top), send_two(bottom)
    acc = own_part(top, bottom, w_out, jnp.stack([two, one, chip, chip]))
    narrow_one, narrow_two = narrow(
        side.reshape(1), main_one, main_two, near_one, near_two, far_one, far_two
    )
    add = lambda *jobs: add_partner(
        core.reshape(1), acc, top_one, bottom_two, narrow_one, narrow_two, jobs
    )
    other, own = 0, 1
    (away_sent,) = add((other, False))
    away_kept, here_sent = add((other, True), (own, False))
    away_top, away_bottom = sum_cores(away_kept, send_core(away_sent))
    from_two, from_one = send_two(away_top), send_one(away_bottom)
    (here_kept,) = add((own, True))
    return last_sum(here_kept, send_core(here_sent), from_two, from_one)


def solution(mesh):
    in_specs = (
        P("seq", "chan"),
        P("seq", "chan"),
        P("seq", "chan"),
        P("seq", "chan"),
        P("chan", None),
    )
    out_specs = P("seq", "chan")
    return jax.shard_map(shards, mesh=mesh, in_specs=in_specs, out_specs=out_specs, check_vma=False)
```

```python
import functools

import jax
import jax.numpy as jnp
import numpy as np
from jax import lax
from jax.experimental import pallas as pl
from jax.experimental.pallas import tpu as pltpu
from jax.sharding import PartitionSpec as P

LANES = 128
COARSE = 128
TOTAL = 2 * COARSE * LANES
PEERS = 32
OWN = 16
SUB = 4
CHIPS = 4
BLOCK = 512
MAIN = 448
TAIL = 32
GROUP = 16
BIG = 56 * 1024 * 1024
SMALL = 24 * 1024 * 1024


def split_bf16(x):
    high = x.astype(jnp.bfloat16)
    low = (x - high.astype(jnp.float32)).astype(jnp.bfloat16)
    return high, low


def tables():
    k = np.arange(COARSE)
    q = np.arange(COARSE)
    r = np.arange(LANES)
    coarse = 2.0 * np.pi * ((k[:, None] * q[None, :]) % (2 * COARSE)) / (2 * COARSE)
    fine = 2.0 * np.pi * ((r[:, None] * r[None, :]) % LANES) / LANES
    twist = 2.0 * np.pi * ((k[:, None] * r[None, :]) % TOTAL) / TOTAL
    middle = 2.0 * np.pi * np.tile((COARSE * r)[None, :], (8, 1)) / TOTAL
    rows = [
        np.concatenate([np.cos(angle), np.sin(angle)], 1) for angle in (coarse, fine, twist, middle)
    ]
    return np.concatenate(rows, 0).astype(np.float32)


def place():
    index = lax.axis_index("chan")
    chip, core = index // 2, index % 2
    step = (1 - 2 * (chip % 2)) * (1 - 2 * core)
    around = lambda n: (chip + CHIPS + n) % CHIPS
    return chip, core, around(step), around(-step), around(2)


def prepare_kernel(
    key_ref, value_ref, taps_ref, w_ref, out_ref, token_ref, same_ref, cross_ref, buffer, arrived
):
    rows, quarter = buffer.shape[1:]
    _, _, gather, reduce, opposite = place()
    start = pl.multiple_of(MAIN + lax.axis_index("seq") % 2 * TAIL, 16)
    copies = []
    for n, column in enumerate((opposite, gather, reduce)):
        at = pl.multiple_of(column * quarter, quarter)
        copies.append(
            pltpu.make_async_copy(
                w_ref.at[pl.ds(start, rows), pl.ds(at, quarter)], buffer.at[n], arrived.at[n]
            )
        )

    @pl.when(pl.program_id(0) == 0)
    def _():
        token_ref[...] = jnp.zeros_like(token_ref)
        for copy in copies:
            copy.start()

    signal = key_ref[...].astype(jnp.float32) * value_ref[...].astype(jnp.float32)
    taps = taps_ref[...]
    for e in range(signal.shape[0] // LANES):
        part = slice(e * LANES, (e + 1) * LANES)
        for s, stream in enumerate((signal, taps)):
            at = (2 * e + s) * OWN
            out_ref[:, at:at + OWN, :] = stream[part, :].T.reshape(PEERS, OWN, LANES)

    @pl.when(pl.program_id(0) == pl.num_programs(0) - 1)
    def _():
        for copy in copies:
            copy.wait()
        both = buffer[0].astype(jnp.float32)
        same_ref[0], cross_ref[0] = both, both
        same_ref[1] = buffer[1].astype(jnp.float32)
        cross_ref[1] = buffer[2].astype(jnp.float32)


def prepare(key_stream, value, taps, w_out):
    rows, channels = key_stream.shape
    quarter = w_out.shape[1] // CHIPS
    steps = 2
    block = pl.BlockSpec((rows // steps, channels), lambda i: (i, 0))
    sent = 2 * SUB * OWN
    tail = jax.ShapeDtypeStruct((2, TAIL, quarter), jnp.float32)
    tail_block = pl.BlockSpec((2, TAIL, quarter), lambda i: (0, 0, 0))
    return pl.pallas_call(
        prepare_kernel,
        grid=(steps,),
        in_specs=[block, block, block, pl.BlockSpec(memory_space=pltpu.HBM)],
        out_specs=(
            pl.BlockSpec((PEERS, sent // steps, LANES), lambda i: (0, i, 0)),
            pl.BlockSpec((8, LANES), lambda i: (0, 0)),
            tail_block,
            tail_block,
        ),
        out_shape=(
            jax.ShapeDtypeStruct((PEERS, sent, LANES), jnp.float32),
            jax.ShapeDtypeStruct((8, LANES), jnp.float32),
            tail,
            tail,
        ),
        scratch_shapes=[
            pltpu.VMEM((3, TAIL, quarter), jnp.bfloat16),
            pltpu.SemaphoreType.DMA((3,)),
        ],
        compiler_params=pltpu.CompilerParams(vmem_limit_bytes=BIG),
        cost_estimate=pl.CostEstimate(flops=0, bytes_accessed=5 << 20, transcendentals=0),
    )(key_stream, value, taps, w_out)


def dot(a, b):
    return jnp.dot(a, b, preferred_element_type=jnp.float32)


def rows_by(a, stacked):
    high, low = split_bf16(a)
    return dot(jnp.concatenate([high, low, high], 1), stacked)


def by_columns(stacked, a):
    high, low = split_bf16(a)
    return dot(stacked, jnp.concatenate([high, low, high], 0))


def multiply(a, b):
    ar, ai, br, bi = a[:, :LANES], a[:, LANES:], b[:, :LANES], b[:, LANES:]
    return jnp.concatenate([ar * br - ai * bi, ar * bi + ai * br], 1)


def convolve_kernel(
    x_ref, table_ref, *refs
):
    out_ref, edge_out, first, second, inverse, last = refs[-6:]
    coarse_at, fine_at, twist_at = [slice(i * COARSE, (i + 1) * COARSE) for i in range(3)]
    edge_at = slice(3 * COARSE, 3 * COARSE + 1)
    cos, sin = table_ref[coarse_at, :LANES], table_ref[coarse_at, LANES:]
    lane = lax.broadcasted_iota(jnp.int32, (COARSE, COARSE), 1)
    weight = jnp.where(lane == 0, 1.0 / TOTAL, 2.0 / TOTAL)
    beside = lambda *parts: jnp.concatenate(parts, 1)
    over = lambda *parts: jnp.concatenate(parts, 0)
    fine_cos, fine_sin = table_ref[fine_at, :LANES], table_ref[fine_at, LANES:]
    for values, table, axis in (
        (over(cos, -sin), first, 1),
        (over(beside(fine_cos, -fine_sin), beside(fine_sin, fine_cos)), second, 0),
        (over(beside(fine_cos, fine_sin), beside(-fine_sin, fine_cos)), inverse, 0),
        (beside(weight * cos, -weight * sin), last, 1),
    ):
        high, low = split_bf16(values)
        table[...] = jnp.concatenate([high, high, low], axis)
    odd = lax.broadcasted_iota(jnp.int32, (COARSE, LANES), 0) % 2
    sign = jnp.where(odd == 0, 1.0 / TOTAL, -1.0 / TOTAL)
    edge = table_ref[edge_at, :]

    half = jnp.zeros((2 * OWN, LANES), jnp.float32)
    for at in range(0, COARSE * 2 * OWN, 4 * OWN):
        half += x_ref[at:at + 2 * OWN, :] - x_ref[at + 2 * OWN:at + 4 * OWN, :]
    edge_cos, edge_sin = edge[:, :LANES], edge[:, LANES:]
    spectrum = rows_by(jnp.concatenate([half * edge_cos, -half * edge_sin], 1), second[...])
    back = rows_by(multiply(spectrum[:OWN], spectrum[OWN:]), inverse[...])
    edge_out[...] = back[:, :LANES] * edge_cos - back[:, LANES:] * edge_sin

    def some_channels(i):
        c0 = GROUP * i
        streams = [
            x_ref[pl.ds(s * OWN + c0 + j, COARSE, stride=2 * OWN), :]
            for j in range(GROUP) for s in range(2)
        ]
        y = by_columns(first[...], jnp.concatenate(streams, 1))
        cos, sin = table_ref[twist_at, :LANES], table_ref[twist_at, LANES:]
        turned = []
        for j in range(2 * GROUP):
            yr = y[:COARSE, j * LANES:(j + 1) * LANES]
            yi = y[COARSE:, j * LANES:(j + 1) * LANES]
            turned.append(jnp.concatenate([yr * cos + yi * sin, yi * cos - yr * sin], 1))
        z = rows_by(jnp.concatenate(turned, 0), second[...])
        products = [
            multiply(
                z[2 * j * COARSE:(2 * j + 1) * COARSE], z[(2 * j + 1) * COARSE:(2 * j + 2) * COARSE]
            )
            for j in range(GROUP)
        ]
        u = rows_by(jnp.concatenate(products, 0), inverse[...])
        columns = []
        for j in range(GROUP):
            ur = u[j * COARSE:(j + 1) * COARSE, :LANES]
            ui = u[j * COARSE:(j + 1) * COARSE, LANES:]
            columns.append(jnp.concatenate([ur * cos - ui * sin, ur * sin + ui * cos], 0))
        result = by_columns(last[...], jnp.concatenate(columns, 1))
        for j in range(GROUP):
            extra = sign * edge_out[pl.ds(c0 + j, 1), :]
            out_ref[pl.ds(c0 + j, COARSE, stride=OWN), :] = (
                result[:, j * LANES:(j + 1) * LANES] + extra
            )

    for i in range(OWN // GROUP):
        some_channels(i)


def convolve(x, *before):
    return pl.pallas_call(
        convolve_kernel,
        in_specs=[pl.BlockSpec()] * 2
        + [pl.BlockSpec(memory_space=pltpu.VMEM)] * len(before),
        out_shape=jax.ShapeDtypeStruct((COARSE * OWN, LANES), jnp.float32),
        scratch_shapes=[
            pltpu.VMEM((OWN, LANES), jnp.float32),
            pltpu.VMEM((2 * COARSE, 3 * COARSE), jnp.bfloat16),
            pltpu.VMEM((6 * LANES, 2 * LANES), jnp.bfloat16),
            pltpu.VMEM((6 * LANES, 2 * LANES), jnp.bfloat16),
            pltpu.VMEM((COARSE, 6 * COARSE), jnp.bfloat16),
        ],
        compiler_params=pltpu.CompilerParams(vmem_limit_bytes=SMALL),
        cost_estimate=pl.CostEstimate(flops=4 << 30, bytes_accessed=4 << 20, transcendentals=0),
    )(x, jnp.asarray(tables()), *before)


def widen_rest_kernel(
    token_ref, w_ref, same_ref, cross_ref, sibling_ref, buffer, wide, arrived, left
):
    channels, quarter = buffer.shape[1:]
    chip, _, gather, reduce, opposite = place()
    half = channels // 2
    copies = []
    for n, column in enumerate((opposite, gather, reduce, chip)):
        at = pl.multiple_of(column * quarter, quarter)
        for h in range(2):
            rows = pl.ds(h * half, half)
            copies.append(
                pltpu.make_async_copy(
                    w_ref.at[rows, pl.ds(at, quarter)], buffer.at[n, rows], arrived.at[2 * n + h]
                )
            )
            copies[-1].start()
    targets = (
        ((same_ref.at[0], MAIN), (cross_ref.at[0], MAIN)),
        ((same_ref.at[1], MAIN), (sibling_ref.at[0], channels)),
        ((cross_ref.at[1], MAIN),),
        ((sibling_ref.at[1], channels),),
    )
    sends = []
    for n, outs in enumerate(targets):
        for h in range(2):
            copies[2 * n + h].wait()
            wide[n, h * half:(h + 1) * half] = buffer[n, h * half:(h + 1) * half].astype(jnp.float32)
            for ref, end in outs:
                rows = pl.ds(h * half, min(end, (h + 1) * half) - h * half)
                sends.append(
                    pltpu.make_async_copy(wide.at[n, rows], ref.at[rows], left.at[len(sends)])
                )
                sends[-1].start()
    for copy in sends:
        copy.wait()


def widen_rest(token, w_out):
    channels, width = w_out.shape
    quarter = width // CHIPS
    shape = lambda rows: jax.ShapeDtypeStruct((2, rows, quarter), jnp.float32)
    anywhere = pl.BlockSpec(memory_space=pl.ANY)
    return pl.pallas_call(
        widen_rest_kernel,
        in_specs=[pl.BlockSpec(memory_space=pltpu.VMEM), pl.BlockSpec(memory_space=pltpu.HBM)],
        out_specs=(anywhere,) * 3,
        out_shape=(shape(MAIN), shape(MAIN), shape(channels)),
        scratch_shapes=[
            pltpu.VMEM((4, channels, quarter), jnp.bfloat16),
            pltpu.VMEM((4, channels, quarter), jnp.float32),
            pltpu.SemaphoreType.DMA((8,)),
            pltpu.SemaphoreType.DMA((12,)),
        ],
        compiler_params=pltpu.CompilerParams(vmem_limit_bytes=BIG),
        cost_estimate=pl.CostEstimate(flops=0, bytes_accessed=15 << 20, transcendentals=0),
    )(token, w_out)


def after_kernel(*refs):
    pass


def after(xs, before):
    anywhere = pl.BlockSpec(memory_space=pl.ANY)
    return pl.pallas_call(
        after_kernel,
        in_specs=[anywhere] * len(xs) + [pl.BlockSpec(memory_space=pltpu.VMEM)] * len(before),
        out_specs=(anywhere,) * len(xs),
        out_shape=tuple(jax.ShapeDtypeStruct(x.shape, x.dtype) for x in xs),
        input_output_aliases={i: i for i in range(len(xs))},
        compiler_params=pltpu.CompilerParams(vmem_limit_bytes=SMALL),
        cost_estimate=pl.CostEstimate(flops=0, bytes_accessed=4096, transcendentals=0),
    )(*xs, *before)


def narrow_tail_kernel(*refs):
    ins, outs = refs[:4], refs[4:]
    side = lax.axis_index("seq") % 2
    for near_ref, far_ref, out_ref in zip(ins[:2], ins[2:], outs):
        for ref, start in ((near_ref, side * TAIL), (far_ref, (1 - side) * TAIL)):
            out_ref[:, pl.ds(pl.multiple_of(start, 16), TAIL), :] = ref[...].astype(jnp.bfloat16)


def narrow_tail(*parts):
    _, rows, quarter = parts[0].shape
    shape = jax.ShapeDtypeStruct((2, 2 * rows, quarter), jnp.bfloat16)
    return pl.pallas_call(
        narrow_tail_kernel,
        out_shape=(shape, shape),
        compiler_params=pltpu.CompilerParams(vmem_limit_bytes=SMALL),
        cost_estimate=pl.CostEstimate(flops=0, bytes_accessed=3 << 20, transcendentals=0),
    )(*parts)


def narrow_kernel(*refs):
    out_ref = refs[-1]
    start = 0
    for ref in refs[:-1]:
        out_ref[start:start + ref.shape[0], :] = ref[...].astype(jnp.bfloat16)
        start += ref.shape[0]


def narrow(*parts):
    quarter = parts[0].shape[2]
    block = lambda rows: pl.BlockSpec((None, rows, quarter), lambda i: (i, 0, 0))
    channels = sum(part.shape[1] for part in parts)
    return pl.pallas_call(
        narrow_kernel,
        grid=(2,),
        in_specs=[block(part.shape[1]) for part in parts],
        out_specs=block(channels),
        out_shape=jax.ShapeDtypeStruct((2, channels, quarter), jnp.bfloat16),
        compiler_params=pltpu.CompilerParams(vmem_limit_bytes=SMALL),
        cost_estimate=pl.CostEstimate(flops=0, bytes_accessed=12 << 20, transcendentals=0),
    )(*parts)


def gate_kernel(conv_ref, query_ref, kept_ref, given_ref):
    _, core, *_ = place()
    half = SUB // 2
    for e in range(SUB):
        i = e % half
        at = core * half + i if e < half else (1 - core) * half + i
        conv = conv_ref[:, pl.ds(pl.multiple_of(at * OWN, OWN), OWN), :]
        conv = conv.reshape(PEERS * OWN, LANES).T
        query = query_ref[pl.ds(pl.multiple_of(at * LANES, LANES), LANES), :]
        gated = query.astype(jnp.float32) * conv
        out_ref = kept_ref if e < half else given_ref
        out_ref[i * LANES:(i + 1) * LANES, :] = gated.astype(jnp.bfloat16).astype(jnp.float32)


def gate(conv, query):
    rows, channels = query.shape
    half = jax.ShapeDtypeStruct((rows // 2, channels), jnp.float32)
    return pl.pallas_call(
        gate_kernel,
        out_shape=(half, half),
        compiler_params=pltpu.CompilerParams(vmem_limit_bytes=SMALL),
        cost_estimate=pl.CostEstimate(flops=0, bytes_accessed=3 << 20, transcendentals=0),
    )(conv, query)


def own_kernel(where_ref, mine_ref, theirs_ref, w_ref, w_other_ref, out_ref):
    mine, theirs = mine_ref[...].astype(jnp.bfloat16), theirs_ref[...].astype(jnp.bfloat16)
    out_ref[...] = dot(mine, w_ref[...]) + dot(theirs, w_other_ref[...].astype(jnp.bfloat16))


def own_part(mine, theirs, w_out, w_other, where):
    rows, channels = mine.shape
    width = w_out.shape[1]
    quarter = width // CHIPS
    return pl.pallas_call(
        own_kernel,
        grid_spec=pltpu.PrefetchScalarGridSpec(
            num_scalar_prefetch=1,
            grid=(2,),
            in_specs=[
                pl.BlockSpec((rows, channels), lambda i, where: (0, 0)),
                pl.BlockSpec((rows, channels), lambda i, where: (0, 0)),
                pl.BlockSpec((channels, quarter), lambda i, where: (0, where[i])),
                pl.BlockSpec((None, channels, quarter), lambda i, where: (i, 0, 0)),
            ],
            out_specs=pl.BlockSpec((None, rows, quarter), lambda i, where: (i, 0, 0)),
        ),
        out_shape=jax.ShapeDtypeStruct((2, rows, quarter), jnp.float32),
        compiler_params=pltpu.CompilerParams(vmem_limit_bytes=SMALL),
        cost_estimate=pl.CostEstimate(flops=1 << 30, bytes_accessed=8 << 20, transcendentals=0),
    )(where, mine, theirs, w_out, w_other)


def add_kernel(which, acc_ref, mine_ref, theirs_ref, w_ref, same_ref, cross_ref):
    _, core, *_ = place()
    mine, theirs = mine_ref[...].astype(jnp.bfloat16), theirs_ref[...].astype(jnp.bfloat16)
    for parity, out_ref in ((core, same_ref), (1 - core, cross_ref)):
        at = pl.ds(pl.multiple_of(parity * BLOCK, BLOCK), BLOCK)
        first, second = w_ref[which, :BLOCK, at], w_ref[which, BLOCK:, at]
        out_ref[...] = acc_ref[which, :, at] + (dot(mine, first) + dot(theirs, second))


def add_partner(acc, mine, theirs, w, which):
    shape = jax.ShapeDtypeStruct((mine.shape[0], BLOCK), jnp.float32)
    in_vmem = pl.BlockSpec(memory_space=pltpu.VMEM)
    return pl.pallas_call(
        functools.partial(add_kernel, which),
        in_specs=[in_vmem] * 4,
        out_specs=(in_vmem, in_vmem),
        out_shape=(shape, shape),
        compiler_params=pltpu.CompilerParams(vmem_limit_bytes=SMALL),
        cost_estimate=pl.CostEstimate(flops=1 << 29, bytes_accessed=4 << 20, transcendentals=0),
    )(acc, mine, theirs, w)


def last_kernel(kept_ref, cross_ref, other_ref, same_ref, out_ref):
    rows = kept_ref.shape[0]
    _, core, *_ = place()
    for half, a_ref, b_ref in ((core, kept_ref, same_ref), (1 - core, other_ref, cross_ref)):
        at = pl.ds(pl.multiple_of(half * rows, rows), rows)
        out_ref[at, :] = (a_ref[...] + b_ref[...]).astype(out_ref.dtype)


def last_sum(kept, cross, other, same):
    rows, columns = kept.shape
    return pl.pallas_call(
        last_kernel,
        out_shape=jax.ShapeDtypeStruct((2 * rows, columns), jnp.bfloat16),
        compiler_params=pltpu.CompilerParams(vmem_limit_bytes=SMALL),
        cost_estimate=pl.CostEstimate(flops=1 << 19, bytes_accessed=4 << 20, transcendentals=0),
    )(kept, cross, other, same)


def send(x, route):
    one = lambda chip: chip ^ 1
    two = lambda chip: (chip - 1 if chip % 2 == 0 else chip + 1) % CHIPS
    pairs = []
    for chip in range(CHIPS):
        for core in range(2):
            gather = lambda c: (one, two)[c](chip)
            reduce = lambda c: (two, one)[c](chip)
            to_chip, to_core = route(chip, core, gather, reduce)
            pairs.append((2 * chip + core, 2 * to_chip + to_core))
    return lax.ppermute(x, "chan", pairs)


def shards(query, key_stream, value, long_filter, w_out):
    send_gather = lambda x: send(x, lambda chip, core, gather, reduce: (gather(core), core))
    send_cross = lambda x: send(x, lambda chip, core, gather, reduce: (gather(1 - core), 1 - core))
    send_core = lambda x: send(x, lambda chip, core, gather, reduce: (chip, 1 - core))
    sum_same = lambda x: send(x, lambda chip, core, gather, reduce: (reduce(core), core))
    sum_cross = lambda x: send(x, lambda chip, core, gather, reduce: (reduce(core), 1 - core))
    send_side = lambda x: lax.ppermute(x, "seq", [(i, i ^ 1) for i in range(PEERS)])
    chip, core, gather, reduce, opposite = place()

    sent, token, tail_same, tail_cross = prepare(key_stream, value, long_filter, w_out)
    near_same, near_cross = send_gather(tail_same), send_cross(tail_cross)
    arrived = [x[0, :8, :LANES] for x in (near_same, near_cross)]
    main_same, main_cross, sibling = widen_rest(token, w_out)
    main_same, main_cross = after((main_same, main_cross), arrived)
    main_same, main_cross = send_gather(main_same), send_cross(main_cross)
    far_same, far_cross = send_side(near_same), send_side(near_cross)
    tails_same, tails_cross = narrow_tail(near_same, near_cross, far_same, far_cross)
    arrived = [x[0, :16, :LANES] for x in (tails_same, tails_cross)]
    w_other = send_core(sibling)
    moved = lax.all_to_all(sent, "seq", split_axis=0, concat_axis=0, tiled=True)
    conv = convolve(
        moved.reshape(PEERS * 2 * SUB * OWN, LANES),
        *arrived,
    )
    home = lax.all_to_all(
        conv.reshape(PEERS, SUB * OWN, LANES), "seq", split_axis=0, concat_axis=0, tiled=True
    )
    mine, given = gate(home, query)
    far_mine, far_theirs = send_gather(mine), send_cross(given)
    theirs = send_core(given)
    acc = own_part(mine, theirs, w_out, w_other, jnp.stack([reduce, chip]))
    w_partner = narrow(main_same, tails_same, main_cross, tails_cross)
    away_same, away_cross = add_partner(acc, far_mine, far_theirs, w_partner, 0)
    from_cross = sum_cross(away_cross)
    from_same = sum_same(away_same)
    kept, other = add_partner(acc, far_mine, far_theirs, w_partner, 1)
    return last_sum(kept, from_cross, send_core(other), from_same)


def solution(mesh):
    in_specs = (
        P("seq", "chan"),
        P("seq", "chan"),
        P("seq", "chan"),
        P("seq", "chan"),
        P("chan", None),
    )
    out_specs = P("seq", "chan")
    return jax.shard_map(shards, mesh=mesh, in_specs=in_specs, out_specs=out_specs, check_vma=False)
```

```python
import functools

import jax
import jax.numpy as jnp
import numpy as np
from jax import lax
from jax.experimental import pallas as pl
from jax.experimental.pallas import tpu as pltpu
from jax.sharding import PartitionSpec as P

LANES = 128
COARSE = 128
TOTAL = 2 * COARSE * LANES
PEERS = 32
OWN = 16
SUB = 4
CHIPS = 4
BLOCK = 512
MAIN = 448
TAIL = 32
GROUP = 16
BIG = 56 * 1024 * 1024
SMALL = 24 * 1024 * 1024


def split_bf16(x):
    high = x.astype(jnp.bfloat16)
    low = (x - high.astype(jnp.float32)).astype(jnp.bfloat16)
    return high, low


def tables():
    k = np.arange(COARSE)
    q = np.arange(COARSE)
    r = np.arange(LANES)
    coarse = 2.0 * np.pi * ((k[:, None] * q[None, :]) % (2 * COARSE)) / (2 * COARSE)
    fine = 2.0 * np.pi * ((r[:, None] * r[None, :]) % LANES) / LANES
    twist = 2.0 * np.pi * ((k[:, None] * r[None, :]) % TOTAL) / TOTAL
    middle = 2.0 * np.pi * np.tile((COARSE * r)[None, :], (8, 1)) / TOTAL
    rows = [
        np.concatenate([np.cos(angle), np.sin(angle)], 1) for angle in (coarse, fine, twist, middle)
    ]
    return np.concatenate(rows, 0).astype(np.float32)


def place():
    index = lax.axis_index("chan")
    chip, core = index // 2, index % 2
    step = (1 - 2 * (chip % 2)) * (1 - 2 * core)
    around = lambda n: (chip + CHIPS + n) % CHIPS
    return chip, core, around(step), around(-step), around(2)


def prepare_kernel(
    key_ref, value_ref, taps_ref, w_ref, out_ref, token_ref, same_ref, cross_ref, buffer, arrived
):
    rows, quarter = buffer.shape[1:]
    _, _, gather, reduce, opposite = place()
    start = pl.multiple_of(MAIN + lax.axis_index("seq") % 2 * TAIL, 16)
    copies = []
    for n, column in enumerate((opposite, gather, reduce)):
        at = pl.multiple_of(column * quarter, quarter)
        copies.append(
            pltpu.make_async_copy(
                w_ref.at[pl.ds(start, rows), pl.ds(at, quarter)], buffer.at[n], arrived.at[n]
            )
        )

    @pl.when(pl.program_id(0) == 0)
    def _():
        token_ref[...] = jnp.zeros_like(token_ref)
        for copy in copies:
            copy.start()

    signal = key_ref[...].astype(jnp.float32) * value_ref[...].astype(jnp.float32)
    taps = taps_ref[...]
    for e in range(signal.shape[0] // LANES):
        part = slice(e * LANES, (e + 1) * LANES)
        for s, stream in enumerate((signal, taps)):
            at = (2 * e + s) * OWN
            out_ref[:, at:at + OWN, :] = stream[part, :].T.reshape(PEERS, OWN, LANES)

    @pl.when(pl.program_id(0) == 0)
    def _():
        for copy in copies:
            copy.wait()
        both = buffer[0].astype(jnp.float32)
        same_ref[0], cross_ref[0] = both, both
        same_ref[1] = buffer[1].astype(jnp.float32)
        cross_ref[1] = buffer[2].astype(jnp.float32)


def prepare(key_stream, value, taps, w_out):
    rows, channels = key_stream.shape
    quarter = w_out.shape[1] // CHIPS
    steps = 2
    block = pl.BlockSpec((rows // steps, channels), lambda i: (i, 0))
    sent = 2 * SUB * OWN
    tail = jax.ShapeDtypeStruct((2, TAIL, quarter), jnp.float32)
    tail_block = pl.BlockSpec((2, TAIL, quarter), lambda i: (0, 0, 0))
    return pl.pallas_call(
        prepare_kernel,
        grid=(steps,),
        in_specs=[block, block, block, pl.BlockSpec(memory_space=pltpu.HBM)],
        out_specs=(
            pl.BlockSpec((PEERS, sent // steps, LANES), lambda i: (0, i, 0)),
            pl.BlockSpec((8, LANES), lambda i: (0, 0)),
            tail_block,
            tail_block,
        ),
        out_shape=(
            jax.ShapeDtypeStruct((PEERS, sent, LANES), jnp.float32),
            jax.ShapeDtypeStruct((8, LANES), jnp.float32),
            tail,
            tail,
        ),
        scratch_shapes=[
            pltpu.VMEM((3, TAIL, quarter), jnp.bfloat16),
            pltpu.SemaphoreType.DMA((3,)),
        ],
        compiler_params=pltpu.CompilerParams(vmem_limit_bytes=BIG),
        cost_estimate=pl.CostEstimate(flops=0, bytes_accessed=5 << 20, transcendentals=0),
    )(key_stream, value, taps, w_out)


def dot(a, b):
    return jnp.dot(a, b, preferred_element_type=jnp.float32)


def rows_by(a, stacked):
    high, low = split_bf16(a)
    return dot(jnp.concatenate([high, low, high], 1), stacked)


def by_columns(stacked, a):
    high, low = split_bf16(a)
    return dot(stacked, jnp.concatenate([high, low, high], 0))


def multiply(a, b):
    ar, ai, br, bi = a[:, :LANES], a[:, LANES:], b[:, :LANES], b[:, LANES:]
    return jnp.concatenate([ar * br - ai * bi, ar * bi + ai * br], 1)


def convolve_kernel(
    x_ref, table_ref, *refs
):
    out_ref, edge_out, first, second, inverse, last = refs[-6:]
    coarse_at, fine_at, twist_at = [slice(i * COARSE, (i + 1) * COARSE) for i in range(3)]
    edge_at = slice(3 * COARSE, 3 * COARSE + 1)
    cos, sin = table_ref[coarse_at, :LANES], table_ref[coarse_at, LANES:]
    lane = lax.broadcasted_iota(jnp.int32, (COARSE, COARSE), 1)
    weight = jnp.where(lane == 0, 1.0 / TOTAL, 2.0 / TOTAL)
    beside = lambda *parts: jnp.concatenate(parts, 1)
    over = lambda *parts: jnp.concatenate(parts, 0)
    fine_cos, fine_sin = table_ref[fine_at, :LANES], table_ref[fine_at, LANES:]
    for values, table, axis in (
        (over(cos, -sin), first, 1),
        (over(beside(fine_cos, -fine_sin), beside(fine_sin, fine_cos)), second, 0),
        (over(beside(fine_cos, fine_sin), beside(-fine_sin, fine_cos)), inverse, 0),
        (beside(weight * cos, -weight * sin), last, 1),
    ):
        high, low = split_bf16(values)
        table[...] = jnp.concatenate([high, high, low], axis)
    odd = lax.broadcasted_iota(jnp.int32, (COARSE, LANES), 0) % 2
    sign = jnp.where(odd == 0, 1.0 / TOTAL, -1.0 / TOTAL)
    edge = table_ref[edge_at, :]

    half = jnp.zeros((2 * OWN, LANES), jnp.float32)
    for at in range(0, COARSE * 2 * OWN, 4 * OWN):
        half += x_ref[at:at + 2 * OWN, :] - x_ref[at + 2 * OWN:at + 4 * OWN, :]
    edge_cos, edge_sin = edge[:, :LANES], edge[:, LANES:]
    spectrum = rows_by(jnp.concatenate([half * edge_cos, -half * edge_sin], 1), second[...])
    back = rows_by(multiply(spectrum[:OWN], spectrum[OWN:]), inverse[...])
    edge_out[...] = back[:, :LANES] * edge_cos - back[:, LANES:] * edge_sin

    def some_channels(i):
        c0 = GROUP * i
        streams = [
            x_ref[pl.ds(s * OWN + c0 + j, COARSE, stride=2 * OWN), :]
            for j in range(GROUP) for s in range(2)
        ]
        y = by_columns(first[...], jnp.concatenate(streams, 1))
        cos, sin = table_ref[twist_at, :LANES], table_ref[twist_at, LANES:]
        turned = []
        for j in range(2 * GROUP):
            yr = y[:COARSE, j * LANES:(j + 1) * LANES]
            yi = y[COARSE:, j * LANES:(j + 1) * LANES]
            turned.append(jnp.concatenate([yr * cos + yi * sin, yi * cos - yr * sin], 1))
        z = rows_by(jnp.concatenate(turned, 0), second[...])
        products = [
            multiply(
                z[2 * j * COARSE:(2 * j + 1) * COARSE], z[(2 * j + 1) * COARSE:(2 * j + 2) * COARSE]
            )
            for j in range(GROUP)
        ]
        u = rows_by(jnp.concatenate(products, 0), inverse[...])
        columns = []
        for j in range(GROUP):
            ur = u[j * COARSE:(j + 1) * COARSE, :LANES]
            ui = u[j * COARSE:(j + 1) * COARSE, LANES:]
            columns.append(jnp.concatenate([ur * cos - ui * sin, ur * sin + ui * cos], 0))
        result = by_columns(last[...], jnp.concatenate(columns, 1))
        for j in range(GROUP):
            extra = sign * edge_out[pl.ds(c0 + j, 1), :]
            out_ref[pl.ds(c0 + j, COARSE, stride=OWN), :] = (
                result[:, j * LANES:(j + 1) * LANES] + extra
            )

    for i in range(OWN // GROUP):
        some_channels(i)


def convolve(x, *before):
    return pl.pallas_call(
        convolve_kernel,
        in_specs=[pl.BlockSpec()] * 2
        + [pl.BlockSpec(memory_space=pltpu.VMEM)] * len(before),
        out_shape=jax.ShapeDtypeStruct((COARSE * OWN, LANES), jnp.float32),
        scratch_shapes=[
            pltpu.VMEM((OWN, LANES), jnp.float32),
            pltpu.VMEM((2 * COARSE, 3 * COARSE), jnp.bfloat16),
            pltpu.VMEM((6 * LANES, 2 * LANES), jnp.bfloat16),
            pltpu.VMEM((6 * LANES, 2 * LANES), jnp.bfloat16),
            pltpu.VMEM((COARSE, 6 * COARSE), jnp.bfloat16),
        ],
        compiler_params=pltpu.CompilerParams(vmem_limit_bytes=SMALL),
        cost_estimate=pl.CostEstimate(flops=4 << 30, bytes_accessed=4 << 20, transcendentals=0),
    )(x, jnp.asarray(tables()), *before)


def widen_rest_kernel(
    token_ref, w_ref, same_ref, cross_ref, sibling_ref, buffer, wide, arrived, left
):
    channels, quarter = buffer.shape[1:]
    chip, _, gather, reduce, opposite = place()
    half = channels // 2
    copies = []
    for n, column in enumerate((opposite, gather, reduce, chip)):
        at = pl.multiple_of(column * quarter, quarter)
        for h in range(2):
            rows = pl.ds(h * half, half)
            copies.append(
                pltpu.make_async_copy(
                    w_ref.at[rows, pl.ds(at, quarter)], buffer.at[n, rows], arrived.at[2 * n + h]
                )
            )
            copies[-1].start()
    targets = (
        ((same_ref.at[0], MAIN), (cross_ref.at[0], MAIN)),
        ((same_ref.at[1], MAIN), (sibling_ref.at[0], channels)),
        ((cross_ref.at[1], MAIN),),
        ((sibling_ref.at[1], channels),),
    )
    sends = []
    for n, outs in enumerate(targets):
        for h in range(2):
            copies[2 * n + h].wait()
            wide[n, h * half:(h + 1) * half] = buffer[n, h * half:(h + 1) * half].astype(jnp.float32)
            for ref, end in outs:
                rows = pl.ds(h * half, min(end, (h + 1) * half) - h * half)
                sends.append(
                    pltpu.make_async_copy(wide.at[n, rows], ref.at[rows], left.at[len(sends)])
                )
                sends[-1].start()
    for copy in sends:
        copy.wait()


def widen_rest(token, w_out):
    channels, width = w_out.shape
    quarter = width // CHIPS
    shape = lambda rows: jax.ShapeDtypeStruct((2, rows, quarter), jnp.float32)
    anywhere = pl.BlockSpec(memory_space=pl.ANY)
    return pl.pallas_call(
        widen_rest_kernel,
        in_specs=[pl.BlockSpec(memory_space=pltpu.VMEM), pl.BlockSpec(memory_space=pltpu.HBM)],
        out_specs=(anywhere,) * 3,
        out_shape=(shape(MAIN), shape(MAIN), shape(channels)),
        scratch_shapes=[
            pltpu.VMEM((4, channels, quarter), jnp.bfloat16),
            pltpu.VMEM((4, channels, quarter), jnp.float32),
            pltpu.SemaphoreType.DMA((8,)),
            pltpu.SemaphoreType.DMA((12,)),
        ],
        compiler_params=pltpu.CompilerParams(vmem_limit_bytes=BIG),
        cost_estimate=pl.CostEstimate(flops=0, bytes_accessed=15 << 20, transcendentals=0),
    )(token, w_out)


def after_kernel(*refs):
    pass


def after(xs, before):
    anywhere = pl.BlockSpec(memory_space=pl.ANY)
    return pl.pallas_call(
        after_kernel,
        in_specs=[anywhere] * len(xs) + [pl.BlockSpec(memory_space=pltpu.VMEM)] * len(before),
        out_specs=(anywhere,) * len(xs),
        out_shape=tuple(jax.ShapeDtypeStruct(x.shape, x.dtype) for x in xs),
        input_output_aliases={i: i for i in range(len(xs))},
        compiler_params=pltpu.CompilerParams(vmem_limit_bytes=SMALL),
        cost_estimate=pl.CostEstimate(flops=0, bytes_accessed=4096, transcendentals=0),
    )(*xs, *before)


def narrow_tail_kernel(*refs):
    ins, outs = refs[:4], refs[4:]
    side = lax.axis_index("seq") % 2
    for near_ref, far_ref, out_ref in zip(ins[:2], ins[2:], outs):
        for ref, start in ((near_ref, side * TAIL), (far_ref, (1 - side) * TAIL)):
            out_ref[:, pl.ds(pl.multiple_of(start, 16), TAIL), :] = ref[...].astype(jnp.bfloat16)


def narrow_tail(*parts):
    _, rows, quarter = parts[0].shape
    shape = jax.ShapeDtypeStruct((2, 2 * rows, quarter), jnp.bfloat16)
    return pl.pallas_call(
        narrow_tail_kernel,
        out_shape=(shape, shape),
        compiler_params=pltpu.CompilerParams(vmem_limit_bytes=SMALL),
        cost_estimate=pl.CostEstimate(flops=0, bytes_accessed=3 << 20, transcendentals=0),
    )(*parts)


def narrow_kernel(*refs):
    out_ref = refs[-1]
    start = 0
    for ref in refs[:-1]:
        out_ref[start:start + ref.shape[0], :] = ref[...].astype(jnp.bfloat16)
        start += ref.shape[0]


def narrow(*parts):
    quarter = parts[0].shape[2]
    block = lambda rows: pl.BlockSpec((None, rows, quarter), lambda i: (i, 0, 0))
    channels = sum(part.shape[1] for part in parts)
    return pl.pallas_call(
        narrow_kernel,
        grid=(2,),
        in_specs=[block(part.shape[1]) for part in parts],
        out_specs=block(channels),
        out_shape=jax.ShapeDtypeStruct((2, channels, quarter), jnp.bfloat16),
        compiler_params=pltpu.CompilerParams(vmem_limit_bytes=SMALL),
        cost_estimate=pl.CostEstimate(flops=0, bytes_accessed=12 << 20, transcendentals=0),
    )(*parts)


def gate_kernel(conv_ref, query_ref, kept_ref, given_ref):
    _, core, *_ = place()
    half = SUB // 2
    for e in range(SUB):
        i = e % half
        at = core * half + i if e < half else (1 - core) * half + i
        conv = conv_ref[:, pl.ds(pl.multiple_of(at * OWN, OWN), OWN), :]
        conv = conv.reshape(PEERS * OWN, LANES).T
        query = query_ref[pl.ds(pl.multiple_of(at * LANES, LANES), LANES), :]
        gated = query.astype(jnp.float32) * conv
        out_ref = kept_ref if e < half else given_ref
        out_ref[i * LANES:(i + 1) * LANES, :] = gated.astype(jnp.bfloat16).astype(jnp.float32)


def gate(conv, query):
    rows, channels = query.shape
    half = jax.ShapeDtypeStruct((rows // 2, channels), jnp.float32)
    return pl.pallas_call(
        gate_kernel,
        out_shape=(half, half),
        compiler_params=pltpu.CompilerParams(vmem_limit_bytes=SMALL),
        cost_estimate=pl.CostEstimate(flops=0, bytes_accessed=3 << 20, transcendentals=0),
    )(conv, query)


def own_kernel(where_ref, mine_ref, theirs_ref, w_ref, w_other_ref, out_ref):
    mine, theirs = mine_ref[...].astype(jnp.bfloat16), theirs_ref[...].astype(jnp.bfloat16)
    out_ref[...] = dot(mine, w_ref[...]) + dot(theirs, w_other_ref[...].astype(jnp.bfloat16))


def own_part(mine, theirs, w_out, w_other, where):
    rows, channels = mine.shape
    width = w_out.shape[1]
    quarter = width // CHIPS
    return pl.pallas_call(
        own_kernel,
        grid_spec=pltpu.PrefetchScalarGridSpec(
            num_scalar_prefetch=1,
            grid=(2,),
            in_specs=[
                pl.BlockSpec((rows, channels), lambda i, where: (0, 0)),
                pl.BlockSpec((rows, channels), lambda i, where: (0, 0)),
                pl.BlockSpec((channels, quarter), lambda i, where: (0, where[i])),
                pl.BlockSpec((None, channels, quarter), lambda i, where: (i, 0, 0)),
            ],
            out_specs=pl.BlockSpec((None, rows, quarter), lambda i, where: (i, 0, 0)),
        ),
        out_shape=jax.ShapeDtypeStruct((2, rows, quarter), jnp.float32),
        compiler_params=pltpu.CompilerParams(vmem_limit_bytes=SMALL),
        cost_estimate=pl.CostEstimate(flops=1 << 30, bytes_accessed=8 << 20, transcendentals=0),
    )(where, mine, theirs, w_out, w_other)


def add_kernel(which, acc_ref, mine_ref, theirs_ref, w_ref, same_ref, cross_ref):
    _, core, *_ = place()
    mine, theirs = mine_ref[...].astype(jnp.bfloat16), theirs_ref[...].astype(jnp.bfloat16)
    for parity, out_ref in ((core, same_ref), (1 - core, cross_ref)):
        at = pl.ds(pl.multiple_of(parity * BLOCK, BLOCK), BLOCK)
        first, second = w_ref[which, :BLOCK, at], w_ref[which, BLOCK:, at]
        out_ref[...] = acc_ref[which, :, at] + (dot(mine, first) + dot(theirs, second))


def add_partner(acc, mine, theirs, w, which):
    shape = jax.ShapeDtypeStruct((mine.shape[0], BLOCK), jnp.float32)
    in_vmem = pl.BlockSpec(memory_space=pltpu.VMEM)
    return pl.pallas_call(
        functools.partial(add_kernel, which),
        in_specs=[in_vmem] * 4,
        out_specs=(in_vmem, in_vmem),
        out_shape=(shape, shape),
        compiler_params=pltpu.CompilerParams(vmem_limit_bytes=SMALL),
        cost_estimate=pl.CostEstimate(flops=1 << 29, bytes_accessed=4 << 20, transcendentals=0),
    )(acc, mine, theirs, w)


def last_kernel(kept_ref, cross_ref, other_ref, same_ref, out_ref):
    rows = kept_ref.shape[0]
    _, core, *_ = place()
    for half, a_ref, b_ref in ((core, kept_ref, same_ref), (1 - core, other_ref, cross_ref)):
        at = pl.ds(pl.multiple_of(half * rows, rows), rows)
        out_ref[at, :] = (a_ref[...] + b_ref[...]).astype(out_ref.dtype)


def last_sum(kept, cross, other, same):
    rows, columns = kept.shape
    return pl.pallas_call(
        last_kernel,
        out_shape=jax.ShapeDtypeStruct((2 * rows, columns), jnp.bfloat16),
        compiler_params=pltpu.CompilerParams(vmem_limit_bytes=SMALL),
        cost_estimate=pl.CostEstimate(flops=1 << 19, bytes_accessed=4 << 20, transcendentals=0),
    )(kept, cross, other, same)


def send(x, route):
    one = lambda chip: chip ^ 1
    two = lambda chip: (chip - 1 if chip % 2 == 0 else chip + 1) % CHIPS
    pairs = []
    for chip in range(CHIPS):
        for core in range(2):
            gather = lambda c: (one, two)[c](chip)
            reduce = lambda c: (two, one)[c](chip)
            to_chip, to_core = route(chip, core, gather, reduce)
            pairs.append((2 * chip + core, 2 * to_chip + to_core))
    return lax.ppermute(x, "chan", pairs)


def shards(query, key_stream, value, long_filter, w_out):
    send_gather = lambda x: send(x, lambda chip, core, gather, reduce: (gather(core), core))
    send_cross = lambda x: send(x, lambda chip, core, gather, reduce: (gather(1 - core), 1 - core))
    send_core = lambda x: send(x, lambda chip, core, gather, reduce: (chip, 1 - core))
    sum_same = lambda x: send(x, lambda chip, core, gather, reduce: (reduce(core), core))
    sum_cross = lambda x: send(x, lambda chip, core, gather, reduce: (reduce(core), 1 - core))
    send_side = lambda x: lax.ppermute(x, "seq", [(i, i ^ 1) for i in range(PEERS)])
    chip, core, gather, reduce, opposite = place()

    sent, token, tail_same, tail_cross = prepare(key_stream, value, long_filter, w_out)
    near_same, near_cross = send_gather(tail_same), send_cross(tail_cross)
    arrived = [x[0, :8, :LANES] for x in (near_same, near_cross)]
    main_same, main_cross, sibling = widen_rest(token, w_out)
    main_same, main_cross = after((main_same, main_cross), arrived)
    main_same, main_cross = send_gather(main_same), send_cross(main_cross)
    far_same, far_cross = send_side(near_same), send_side(near_cross)
    tails_same, tails_cross = narrow_tail(near_same, near_cross, far_same, far_cross)
    arrived = [x[0, :16, :LANES] for x in (tails_same, tails_cross)]
    w_other = send_core(sibling)
    moved = lax.all_to_all(sent, "seq", split_axis=0, concat_axis=0, tiled=True)
    conv = convolve(
        moved.reshape(PEERS * 2 * SUB * OWN, LANES),
        *arrived,
    )
    home = lax.all_to_all(
        conv.reshape(PEERS, SUB * OWN, LANES), "seq", split_axis=0, concat_axis=0, tiled=True
    )
    mine, given = gate(home, query)
    far_mine, far_theirs = send_gather(mine), send_cross(given)
    theirs = send_core(given)
    acc = own_part(mine, theirs, w_out, w_other, jnp.stack([reduce, chip]))
    w_partner = narrow(main_same, tails_same, main_cross, tails_cross)
    away_same, away_cross = add_partner(acc, far_mine, far_theirs, w_partner, 0)
    from_cross = sum_cross(away_cross)
    from_same = sum_same(away_same)
    kept, other = add_partner(acc, far_mine, far_theirs, w_partner, 1)
    return last_sum(kept, from_cross, send_core(other), from_same)


def solution(mesh):
    in_specs = (
        P("seq", "chan"),
        P("seq", "chan"),
        P("seq", "chan"),
        P("seq", "chan"),
        P("chan", None),
    )
    out_specs = P("seq", "chan")
    return jax.shard_map(shards, mesh=mesh, in_specs=in_specs, out_specs=out_specs, check_vma=False)
```
